256 devices in a mesh: blk: 16 (over z_hi, y, core), tp: 16 (over z_lo, x).
Axes of the slice: x: 4, y: 4, z: 8 (z_hi: 2, z_lo: 4; z = z_hi * 4 + z_lo), core: 2. Of those that a mesh axis runs over, the one named last changes fastest.
Arguments:
- hidden_in: bfloat16 [8192, 4096], P('blk', 'tp'), may hold values from -16 to 16
- w_query: bfloat16 [4096, 4096], P(None, 'tp'), may hold values from -0.09375 to 0.09375
- w_keyval: bfloat16 [4096, 2048], P('tp'), may hold values from -0.09375 to 0.09375
- routing: int32 [16, 1], replicated, may hold values from 0 to 3; in each aligned block of 16 rows (0 to 15, 16 to 31, ...) at most 8 rows name the same one
- hosts: int32 [16], replicated, may hold values from 0 to 15, each once
Outputs:
- attended: bfloat16 [8192, 4096], P('blk', 'tp')
- decode_cache: bfloat16 [16, 8, 512, 2048], P('blk', None, None, 'tp')
The draws below stay inside these ranges and needn't reach their ends.
Inputs may be any that keep to these rules, and one draw needn't show every extreme that they name: `routing`: each prompt block names one decode instance; each of the 4 instances is named by at least one block and by at most 8, a bound that some instance reaches. `hosts`: A permutation of the 16 instance ids; only the first 4 entries are used.
All inputs are finite; a program needn't handle non-finite values.
Results may differ from the reference program's by a relative error of at most 0.007.
The reference program's roundings to bfloat16 on the way count: a program that leaves them out, or rounds other values in their place, can miss the bound.
Values may be sent and summed in bfloat16 or wider, within the bound.
A program may use at most 128 MiB of HBM per device.

```python
import math
import jax
import jax.numpy as jnp
import numpy as np
from jax import lax

D = 4096
HEADS = 32
KVH = 8
HD = 128
TOK_DEV = 512
DECODE = 4
BLOCKS = 16
SEQ = 8192
CAP = 8


def draw_hidden_in(key, part):
    key = jax.random.fold_in(key, 11)
    base_key = jax.random.fold_in(key, 0)
    base = jax.random.normal(base_key, (SEQ, D), jnp.float32)
    values = jnp.clip(base, -6.0, 6.0)
    return values.astype(jnp.bfloat16)


def steps_of(own_key, extent, cuts, low, top_value):
    loudness = 1.0
    for dim, parts in cuts:
        heights = jax.random.uniform(jax.random.fold_in(jax.random.fold_in(own_key, 6), dim), (parts,), jnp.float32, low / len(cuts), top_value / len(cuts))
        loudness = loudness * jnp.repeat(jnp.exp(heights), extent[dim] // parts).reshape((-1,) + (1,) * (len(extent) - 1 - dim))
    return loudness


def shared_out(rng, own, number, rows, amount, top, most, lean):
    ranking = jax.random.permutation(rng, amount)
    crowded, ordinary = shares(amount, rows * top, most, lean, True), shares(amount, rows * top, most, lean, False)
    places = jnp.arange(amount)

    def named(sizes, turn):
        used = int((sizes > 0).sum())
        fixed = max(1, used // 4)
        passed = fixed + (places - fixed + turn * (used - fixed)) % max(1, amount - fixed)
        return jnp.zeros((amount,), jnp.int32).at[ranking[jnp.where(places < fixed, places, passed)]].set(jnp.asarray(sizes, jnp.int32))

    sizes = jnp.where(number % 4 == 0, named(crowded, number // 4), named(ordinary, number - number // 4 - 1))
    mixed = jax.random.permutation(jax.random.fold_in(own, 3), amount)
    donor, taker = mixed[0:amount // 2 * 2:2], mixed[1:amount // 2 * 2:2]
    room = jnp.minimum(sizes[donor] - 1, most - sizes[taker]) // 2
    room = jnp.where((donor == ranking[0]) | (taker == ranking[0]) | (sizes[taker] == 0), 0, jnp.maximum(room, 0))
    passed = jax.random.randint(jax.random.fold_in(own, 4), (amount // 2,), 0, 1 << 20) % (room + 1)
    sizes = sizes.at[donor].add(-passed).at[taker].add(passed)
    items = jnp.searchsorted(jnp.cumsum(sizes), jnp.arange(rows * top), side="right").astype(jnp.int32)
    table = items.reshape(top, rows).T
    table = table[jax.random.permutation(jax.random.fold_in(own, 1), rows)]
    turn = jax.random.randint(jax.random.fold_in(own, 2), (rows, 1), 0, top)
    return jnp.take_along_axis(table, (jnp.arange(top)[None, :] + turn) % top, axis=1)


def shares(number_of, total, limit, slope, full):
    loads = [(1 << 20) // math.isqrt(standing ** slope) + 1 for standing in range(1, number_of + 1)]
    largest = limit if full else min(limit, max(-(-total // number_of), total * loads[0] // sum(loads)))
    least = 1 if total - largest >= number_of - 1 else 0
    holding, surplus = [largest] + [least] * (number_of - 1), total - largest - least * (number_of - 1)
    while surplus > 0:
        candidates = [i for i in range(1, number_of) if holding[i] < largest] or [i for i in range(1, number_of) if holding[i] < limit]
        pool, remaining = sum([loads[i] for i in candidates]), surplus
        for i in candidates:
            extra = min(limit - holding[i], max(1, remaining * loads[i] // pool), surplus)
            holding[i] = holding[i] + extra
            surplus = surplus - extra
    return np.array(holding)


def noise(own_key, shape, deviation, reach, cuts=(), kind=jnp.bfloat16):
    level = steps_of(own_key, shape, cuts, -0.22, 0.18) if cuts else 1.0
    result = jax.random.normal(own_key, shape, jnp.float32) * deviation * level
    return jnp.minimum(jnp.maximum(result, -reach), reach).astype(kind)


def setup_inputs(seed: int = 0) -> dict:
    key_of = jax.random.split(jax.random.key(seed), 6)
    hidden_in = draw_hidden_in(jax.random.fold_in(key_of[5], 71), 0)
    w_query = noise(key_of[1], (D, HEADS * HD), D ** -0.5, 0.09375, ((1, 16),))
    w_keyval = noise(key_of[2], (D, 2 * KVH * HD), D ** -0.5, 0.09375, ((0, 16),))
    routing_keys = jax.random.split(jax.random.fold_in(key_of[3], 1), BLOCKS // BLOCKS)
    routing_turns = jax.random.permutation(jax.random.fold_in(key_of[3], 3), BLOCKS // BLOCKS)
    routing = jax.vmap(lambda own, number: shared_out(jax.random.fold_in(key_of[3], 2), own, number, BLOCKS, DECODE, 1, CAP, 2))(routing_keys, routing_turns).reshape((BLOCKS, 1))
    hosts = jax.random.permutation(key_of[4], BLOCKS).astype(jnp.int32)
    return dict(hidden_in=hidden_in, w_query=w_query, w_keyval=w_keyval, routing=routing, hosts=hosts)


def reference(hidden_in, w_query, w_keyval, routing, hosts):
    query = jnp.dot(hidden_in, w_query, preferred_element_type=jnp.float32).astype(jnp.bfloat16)
    keyval = jnp.dot(hidden_in, w_keyval, preferred_element_type=jnp.float32).astype(jnp.bfloat16)
    group_size = HEADS // KVH
    queries = query.reshape(SEQ, KVH, group_size, HD).astype(jnp.float32)
    kv_pairs = keyval.reshape(SEQ, KVH, 2, HD).astype(jnp.float32)
    score_scale = HD ** -0.5
    key_pos = jnp.arange(SEQ, dtype=jnp.int32)

    def one_head(head_id):
        head_q = queries[:, head_id]
        key_rows = kv_pairs[:, head_id, 0]
        value_rows = kv_pairs[:, head_id, 1]

        def one_block(block_id):
            block_q = lax.dynamic_slice_in_dim(head_q, block_id * TOK_DEV, TOK_DEV, 0)
            scores = jnp.einsum("tgd,nd->gtn", block_q, key_rows) * score_scale
            q_pos = block_id * TOK_DEV + jnp.arange(TOK_DEV, dtype=jnp.int32)
            allowed = key_pos[None, :] <= q_pos[:, None]
            largest = jnp.max(jnp.where(allowed, scores, -1e30), axis=-1)
            weights = jnp.where(allowed, jnp.exp(scores - largest[..., None]), 0.0)
            summed = jnp.sum(weights, axis=-1)
            rounded = lax.optimization_barrier(weights.astype(jnp.bfloat16))
            numer = jnp.einsum("gtn,nd->gtd", rounded.astype(jnp.float32), value_rows)
            return jnp.transpose(numer / summed[..., None], (1, 0, 2))

        return lax.map(one_block, jnp.arange(BLOCKS, dtype=jnp.int32))

    heads_out = lax.map(one_head, jnp.arange(KVH, dtype=jnp.int32))
    attended = jnp.transpose(heads_out, (1, 2, 0, 3, 4)).reshape(SEQ, HEADS * HD).astype(jnp.bfloat16)

    assigned = routing[:, 0]
    block_ids = jnp.arange(BLOCKS, dtype=jnp.int32)
    earlier = (assigned[:, None] == assigned[None, :]) & (block_ids[None, :] < block_ids[:, None])
    slot_of = jnp.sum(earlier.astype(jnp.int32), axis=1)
    owners = hosts[assigned]
    block_data = keyval.reshape(BLOCKS, TOK_DEV, 2 * KVH * HD).astype(jnp.float32)
    slot_ids = jnp.arange(CAP, dtype=jnp.int32)

    def host_cache(host_id):
        select = ((owners == host_id)[None, :] & (slot_of[None, :] == slot_ids[:, None])).astype(jnp.float32)
        return jnp.einsum("sb,btw->stw", select, block_data).astype(jnp.bfloat16)

    decode_cache = lax.map(host_cache, block_ids)
    return attended, decode_cache
```

```python
import functools

import jax
import jax.numpy as jnp
from jax import lax
from jax.experimental import pallas as pl
from jax.experimental.pallas import tpu as pltpu
from jax.sharding import PartitionSpec as P

HEADS = 32
KVH = 8
HD = 128
TOK = 512
CAP = 8
NB = 16
NT = 16
FD = 256
PART = 32
R = 2
RC = TOK // R
HC = RC // 2
TQ = 256
MESH = pl.DeviceIdType.MESH
LOG2E = 1.4426950408889634
SCALE2 = HD**-0.5 * LOG2E
NEG = -1e30


def kernel(
    hidden_ref, wq_ref, wkv_ref, routing_ref, hosts_ref,
    att_ref, cache_ref,
    hid, wq, wkv, kv, tmp, acc, qbuf, sbuf, cbuf,
    loc_sem, z_recv, z_send, x_recv, x_send,
    w_recv, w_send, wy_recv, wy_send, ws_recv, ws_send,
    y_recv, y_send, s_recv, s_send, t_recv, t_send, c_recv, c_send,
):
    b = lax.axis_index("blk")
    t = lax.axis_index("tp")
    c, y, h = b % 2, (b // 2) % 4, b // 8
    x, z = t % 4, t // 4
    part = b % 8
    xr, xl = (x + 1) % 4, (x + 3) % 4
    yr, yl, yo = (y + 1) % 4, (y + 3) % 4, (y + 2) % 4
    dev_xr, dev_xl = (b, z * 4 + xr), (b, z * 4 + xl)
    dev_yr, dev_yl = (h * 8 + yr * 2 + c, t), (h * 8 + yl * 2 + c, t)
    dev_sib = (b + 1 - 2 * c, t)
    zfar = (z + 2) % 4
    zhigh = z // 2
    h_up = (h + zhigh) % 2
    h_dn = (h + 1 - zhigh) % 2
    dev_up = (h_up * 8 + y * 2 + c, zfar * 4 + x)
    dev_dn = (h_dn * 8 + y * 2 + c, zfar * 4 + x)

    def rcopy(src, dst, ssem, rsem, dev):
        return pltpu.make_async_remote_copy(
            src_ref=src, dst_ref=dst, send_sem=ssem, recv_sem=rsem, device_id=dev, device_id_type=MESH
        )

    own_hid = pltpu.make_async_copy(hidden_ref, hid.at[z, x], loc_sem.at[0])
    own_hid.start()
    load_wq = pltpu.make_async_copy(wq_ref, wq, loc_sem.at[1])
    load_wq.start()

    barrier = pltpu.get_barrier_semaphore()

    def greet(dev):
        pl.semaphore_signal(barrier, inc=1, device_id=dev, device_id_type=MESH)

    def greet_tp(i, carry):
        greet((b, (t + i) % NT))
        return carry

    lax.fori_loop(1, NT, greet_tp, 0)
    for dev in (dev_yr, dev_yl, dev_sib, dev_up, dev_dn):
        greet(dev)
    pl.semaphore_wait(barrier, NT - 1 + 5)

    def rows(r):
        return pl.ds(r * RC, RC)

    def zk(k):
        return (z, z + 1 - 2 * (z % 2), 2 - z // 2, 3 - 3 * (z // 2))[k]

    def z_copy(r, zp, up):
        ref = hid.at[zp, x, rows(r)]
        g = r * 4 + zp
        to = (b, t + 4) if up else (b, t - 4)
        return rcopy(ref, ref, z_send.at[0 if up else 1, g], z_recv.at[g], to)

    def x_copy(r, zp, kind):
        g = r * 4 + zp
        if kind == 0:
            ref, to = hid.at[zp, x, rows(r)], dev_xr
        elif kind == 1:
            ref, to = hid.at[zp, x, rows(r)], dev_xl
        elif kind == 2:
            ref, to = hid.at[zp, xl, pl.ds(r * RC, HC)], dev_xr
        else:
            ref, to = hid.at[zp, xr, pl.ds(r * RC + HC, HC)], dev_xl
        return rcopy(ref, ref, x_send.at[kind, g], x_recv.at[kind, g], to)

    def x_wait(r, zp, kind):
        g = r * 4 + zp
        if kind == 0:
            ref, to = hid.at[zp, xl, rows(r)], dev_xl
        elif kind == 1:
            ref, to = hid.at[zp, xr, rows(r)], dev_xr
        elif kind == 2:
            ref, to = hid.at[zp, (x + 2) % 4, pl.ds(r * RC, HC)], dev_xl
        else:
            ref, to = hid.at[zp, (x + 2) % 4, pl.ds(r * RC + HC, HC)], dev_xr
        rcopy(ref, ref, x_send.at[kind, g], x_recv.at[kind, g], to).wait_recv()

    def a_send(n):
        r, k = n // 4, n % 4
        zp = zk(k)
        if k > 0:
            ref = hid.at[zp, x, rows(r)]
            g = r * 4 + zp
            rcopy(ref, ref, z_send.at[0, g], z_recv.at[g], dev_xr).wait_recv()
        x_copy(r, zp, 0).start()
        x_copy(r, zp, 1).start()

        @pl.when((z < 3) & (zp <= z))
        def _():
            z_copy(r, zp, True).start()

        @pl.when((z > 0) & (zp >= z))
        def _():
            z_copy(r, zp, False).start()

    def a_forward(n):
        r, k = n // 4, n % 4
        zp = zk(k)
        x_wait(r, zp, 0)
        x_copy(r, zp, 2).start()
        x_wait(r, zp, 1)
        x_copy(r, zp, 3).start()

    def a_finish(n):
        r, k = n // 4, n % 4
        zp = zk(k)
        x_wait(r, zp, 2)
        x_wait(r, zp, 3)

    def a_drain():
        for r in range(R):
            for zp in range(4):
                for kind in range(4):
                    x_copy(r, zp, kind).wait_send()

                @pl.when((z < 3) & (zp <= z))
                def _():
                    z_copy(r, zp, True).wait_send()

                @pl.when((z > 0) & (zp >= z))
                def _():
                    z_copy(r, zp, False).wait_send()

    def w_start():
        src_rows = pl.ds(part * PART, PART)

        def one(i, carry):
            to = (t + i) % NT
            rcopy(
                wkv_ref.at[src_rows, pl.ds(pl.multiple_of((to // 2) * 2 * HD, 2 * HD), 2 * HD)],
                wkv.at[t, part], w_send.at[0], w_recv.at[0], (b, to),
            ).start()
            return carry

        pltpu.make_async_copy(
            wkv_ref.at[src_rows, pl.ds(pl.multiple_of((t // 2) * 2 * HD, 2 * HD), 2 * HD)],
            wkv.at[t, part], w_recv.at[0],
        ).start()
        lax.fori_loop(1, NT, one, 0)

    def w_ref(p):
        return wkv.at[:, p]

    def w_copy(kind):
        if kind == 0:
            ref, to = wkv.at[:, part], dev_yr
        elif kind == 1:
            ref, to = wkv.at[:, part], dev_yl
        elif kind == 2:
            ref, to = wkv.at[pl.ds(0, 8), yl * 2 + c], dev_yr
        else:
            ref, to = wkv.at[pl.ds(8, 8), yr * 2 + c], dev_yl
        return rcopy(ref, ref, wy_send.at[kind], wy_recv.at[kind], to)

    def w_wait(kind):
        if kind == 0:
            ref = wkv.at[:, yl * 2 + c]
        elif kind == 1:
            ref = wkv.at[:, yr * 2 + c]
        elif kind == 2:
            ref = wkv.at[pl.ds(0, 8), yo * 2 + c]
        else:
            ref = wkv.at[pl.ds(8, 8), yo * 2 + c]
        rcopy(ref, ref, wy_send.at[kind], wy_recv.at[kind], dev_yl).wait_recv()

    def w_sib(i, mine=True):
        yy = (y, yl, yr, yo)[i]
        ref = wkv.at[:, yy * 2 + (c if mine else 1 - c)]
        return rcopy(ref, ref, ws_send.at[i], ws_recv.at[i], dev_sib)

    def w_step(i):
        if i == 0:
            ref = wkv.at[:, part]
            rcopy(ref, ref, w_send.at[0], w_recv.at[0], dev_xr).wait_recv()
            w_copy(0).start()
            w_copy(1).start()
            w_sib(0).start()
        elif i == 1:
            w_wait(0)
            w_copy(2).start()
            w_sib(1).start()
            w_wait(1)
            w_copy(3).start()
            w_sib(2).start()
        elif i == 2:
            w_wait(2)
            w_wait(3)
            w_sib(3).start()
        else:
            for j in range(4):
                w_sib(j, False).wait_recv()

    def w_drain():
        ref = wkv.at[pl.ds(0, NT - 1), part]
        rcopy(ref, ref, w_send.at[0], w_recv.at[0], dev_xr).wait_send()
        for j in range(4):
            w_copy(j).wait_send()
            w_sib(j).wait_send()

    def project(r):
        acc[...] = jnp.zeros_like(acc)

        def body(zp, carry):
            for half in range(2):
                total = None
                for xp in range(4):
                    rhs = wq[zp * 4 + xp] if half == 0 else wkv[zp * 4 + xp].reshape(FD, 2 * HD)
                    one = jnp.dot(hid[zp, xp, rows(r)], rhs, preferred_element_type=jnp.float32)
                    total = one if total is None else total + one
                acc[half] += total
            return carry

        lax.fori_loop(0, 4, body, 0)
        qbuf[rows(r)] = acc[0].astype(jnp.bfloat16)
        kv[b, rows(r)] = acc[1].astype(jnp.bfloat16)

    def kv_block(far, yy, cc):
        return ((h + far) % 2) * 8 + yy * 2 + cc

    def b_copy(r, far, kind):
        if kind == 0:
            ref, to = kv.at[kv_block(far, y, c), rows(r)], dev_yr
        elif kind == 1:
            ref, to = kv.at[kv_block(far, y, c), rows(r)], dev_yl
        elif kind == 2:
            ref, to = kv.at[kv_block(far, yl, c), pl.ds(r * RC, HC)], dev_yr
        else:
            ref, to = kv.at[kv_block(far, yr, c), pl.ds(r * RC + HC, HC)], dev_yl
        g = r * 2 + far
        return rcopy(ref, ref, y_send.at[kind, g], y_recv.at[kind, g], to)

    def b_wait(r, far, kind):
        if kind == 0:
            ref = kv.at[kv_block(far, yl, c), rows(r)]
        elif kind == 1:
            ref = kv.at[kv_block(far, yr, c), rows(r)]
        elif kind == 2:
            ref = kv.at[kv_block(far, yo, c), pl.ds(r * RC, HC)]
        else:
            ref = kv.at[kv_block(far, yo, c), pl.ds(r * RC + HC, HC)]
        g = r * 2 + far
        rcopy(ref, ref, y_send.at[kind, g], y_recv.at[kind, g], dev_yl).wait_recv()

    def b_sib(r, far, i, mine=True):
        yy = (y, yl, yr, yo)[i]
        ref = kv.at[kv_block(far, yy, c if mine else 1 - c), rows(r)]
        g = r * 2 + far
        return rcopy(ref, ref, s_send.at[i, g], s_recv.at[i, g], dev_sib)

    def cross_first(r, way):
        src = kv.at[b, pl.ds(r * RC + way * HC, HC)]
        return rcopy(
            src, tmp.at[r, way], t_send.at[r, way], t_recv.at[r, way], (dev_up, dev_dn)[way]
        )

    def cross_second(r, way):
        hs = (h_dn, h_up)[way]
        dst = kv.at[hs * 8 + y * 2 + c, pl.ds(r * RC + way * HC, HC)]
        return rcopy(
            tmp.at[r, way], dst, c_send.at[r, way], c_recv.at[r, way], (dev_up, dev_dn)[way]
        )

    def cross_wait(r, way):
        dst = kv.at[kv_block(1, y, c), pl.ds(r * RC + way * HC, HC)]
        rcopy(
            tmp.at[r, way], dst, c_send.at[r, way], c_recv.at[r, way], (dev_up, dev_dn)[way]
        ).wait_recv()

    def b_step(r, i):
        if i == 0:
            for way in range(2):
                cross_first(r, way).start()
            b_copy(r, 0, 0).start()
            b_copy(r, 0, 1).start()
            b_sib(r, 0, 0).start()
        elif i == 1:
            for way in range(2):
                cross_first(r, way).wait_recv()
                cross_second(r, way).start()
            b_forward(r, 0)
        elif i == 2:
            b_finish(r, 0)
            for way in range(2):
                cross_wait(r, way)
            b_copy(r, 1, 0).start()
            b_copy(r, 1, 1).start()
            b_sib(r, 1, 0).start()
        elif i == 3:
            b_forward(r, 1)
        elif i == 4:
            b_finish(r, 1)
        else:
            for far in range(2):
                for j in range(4):
                    b_sib(r, far, j, False).wait_recv()

    def b_forward(r, far):
        b_wait(r, far, 0)
        b_copy(r, far, 2).start()
        b_sib(r, far, 1).start()
        b_wait(r, far, 1)
        b_copy(r, far, 3).start()
        b_sib(r, far, 2).start()

    def b_finish(r, far):
        b_wait(r, far, 2)
        b_wait(r, far, 3)
        b_sib(r, far, 3).start()

    def b_drain():
        for r in range(R):
            for far in range(2):
                for j in range(4):
                    b_copy(r, far, j).wait_send()
                    b_sib(r, far, j).wait_send()
            for way in range(2):
                cross_first(r, way).wait_send()
                cross_second(r, way).wait_send()

    own_hid.wait()
    for n in range(4 * R + 6):
        if n < 4 * R:
            a_send(n)
        if n == 0:
            w_start()
        if 1 <= n <= 4 * R:
            a_forward(n - 1)
        if 2 <= n <= 4 * R + 1:
            a_finish(n - 2)
        if 1 <= n <= 3:
            w_step(n - 1)
        if n == 5:
            w_step(3)
            load_wq.wait()
        if n >= 5 and (n - 5) % 4 == 0 and n < 4 * R + 5:
            project((n - 5) // 4)
        for r in range(R):
            i = n - (4 * r + 5)
            if 0 <= i <= 4:
                b_step(r, i)
    for r in range(R):
        b_step(r, 5)

    count = jnp.int32(0)
    index = [jnp.int32(0)] * CAP
    for bb in range(NB):
        hit = hosts_ref[routing_ref[bb]] == b
        for s in range(CAP):
            index[s] = jnp.where(hit & (count == s), bb, index[s])
        count = count + hit.astype(jnp.int32)
    for s in range(CAP):
        @pl.when(t % 2 == 0)
        def _():
            cbuf[s] = jnp.where(s < count, kv[index[s], :, 0:HD], jnp.zeros((TOK, HD), jnp.bfloat16))

        @pl.when(t % 2 == 1)
        def _():
            cbuf[s] = jnp.where(s < count, kv[index[s], :, HD:], jnp.zeros((TOK, HD), jnp.bfloat16))
    store_cache = pltpu.make_async_copy(cbuf, cache_ref, loc_sem.at[2])
    store_cache.start()

    lanes = TOK // HD

    def lane_max(m, s):
        for i in range(lanes):
            m = jnp.maximum(m, s[:, i * HD : (i + 1) * HD])
        return m

    def q_tile(i, carry):
        r0 = pl.multiple_of(i * TQ, TQ)
        q = jnp.concatenate([qbuf[pl.ds(r0, TQ), 0:HD], qbuf[pl.ds(r0, TQ), HD:]], axis=0)

        def scores(kb):
            return lax.dot_general(
                q, kv[kb, :, 0:HD], (((1,), (1,)), ((), ())), preferred_element_type=jnp.float32
            )

        def first(kb, m):
            s = scores(kb)
            sbuf[kb] = s
            return lane_max(m, s)

        m = lax.fori_loop(0, b, first, jnp.full((2 * TQ, HD), NEG, jnp.float32))
        s = scores(b)
        row = lax.broadcasted_iota(jnp.int32, (2 * TQ, TOK), 0) % TQ + r0
        col = lax.broadcasted_iota(jnp.int32, (2 * TQ, TOK), 1)
        s = jnp.where(col <= row, s, NEG)
        sbuf[b] = s
        m = jnp.max(lane_max(m, s), axis=1, keepdims=True) * SCALE2

        def second(kb, state):
            total, out = state
            p = jnp.exp2(sbuf[kb] * SCALE2 - m)
            for j in range(lanes):
                total = total + p[:, j * HD : (j + 1) * HD]
            out = out + jnp.dot(
                p.astype(jnp.bfloat16), kv[kb, :, HD:], preferred_element_type=jnp.float32
            )
            return total, out

        zero = jnp.zeros((2 * TQ, HD), jnp.float32)
        total, out = lax.fori_loop(0, b + 1, second, (zero, zero))
        out = (out / jnp.sum(total, axis=1, keepdims=True)).astype(jnp.bfloat16)
        att_ref[pl.ds(r0, TQ), 0:HD] = out[:TQ]
        att_ref[pl.ds(r0, TQ), HD:] = out[TQ:]
        return carry

    lax.fori_loop(0, TOK // TQ, q_tile, 0)

    a_drain()
    w_drain()
    b_drain()
    store_cache.wait()


def local(hidden_in, w_query, w_keyval, routing, hosts):
    any_spec = pl.BlockSpec(memory_space=pl.ANY)
    smem = pl.BlockSpec(memory_space=pltpu.SMEM)
    dma = pltpu.SemaphoreType.DMA
    bf16, f32 = jnp.bfloat16, jnp.float32
    attended, cache = pl.pallas_call(
        kernel,
        out_shape=(
            jax.ShapeDtypeStruct((TOK, 2 * HD), bf16),
            jax.ShapeDtypeStruct((CAP, TOK, HD), bf16),
        ),
        in_specs=[any_spec, any_spec, any_spec, smem, smem],
        out_specs=(pl.BlockSpec(memory_space=pltpu.VMEM), any_spec),
        scratch_shapes=[
            pltpu.VMEM((4, 4, TOK, FD), bf16),
            pltpu.VMEM((NT, FD, 2 * HD), bf16),
            pltpu.VMEM((NT, 8, PART, 2 * HD), bf16),
            pltpu.VMEM((NB, TOK, 2 * HD), bf16),
            pltpu.VMEM((R, 2, HC, 2 * HD), bf16),
            pltpu.VMEM((2, RC, 2 * HD), f32),
            pltpu.VMEM((TOK, 2 * HD), bf16),
            pltpu.VMEM((NB, 2 * TQ, TOK), f32),
            pltpu.VMEM((CAP, TOK, HD), bf16),
            dma((3,)),
            dma((4 * R,)), dma((2, 4 * R)),
            dma((4, 4 * R)), dma((4, 4 * R)),
            dma((1,)), dma((1,)),
            dma((4,)), dma((4,)),
            dma((4,)), dma((4,)),
            dma((4, 2 * R)), dma((4, 2 * R)),
            dma((4, 2 * R)), dma((4, 2 * R)),
            dma((R, 2)), dma((R, 2)),
            dma((R, 2)), dma((R, 2)),
        ],
        compiler_params=pltpu.CompilerParams(
            collective_id=0, has_side_effects=True, vmem_limit_bytes=56 * 1024 * 1024
        ),
        cost_estimate=pl.CostEstimate(flops=8 * 10**9, bytes_accessed=8 * 2**20, transcendentals=8 * 2**20),
    )(hidden_in, w_query.reshape(NT, FD, 2 * HD), w_keyval, routing.reshape(NB), hosts)
    return attended, cache[None]


def solution(mesh):
    in_specs = (P("blk", "tp"), P(None, "tp"), P("tp", None), P(), P())
    out_specs = (P("blk", "tp"), P("blk", None, None, "tp"))
    return jax.shard_map(local, mesh=mesh, in_specs=in_specs, out_specs=out_specs, check_vma=False)
```

```python
import functools

import jax
import jax.numpy as jnp
from jax import lax
from jax.experimental import pallas as pl
from jax.experimental.pallas import tpu as pltpu
from jax.sharding import PartitionSpec as P

HEADS = 32
KVH = 8
HD = 128
TOK = 512
CAP = 8
NB = 16
NT = 16
FD = 256
PART = 32
R = 4
RC = TOK // R
HC = RC // 2
TILE = 2 * TOK // 2
QUAD = 4
MESH = pl.DeviceIdType.MESH
LOG2E = 1.4426950408889634
SCALE2 = HD**-0.5 * LOG2E
NEG = -1e30

XSEQ = [
    (0, 0), (1, 0), (0, 1), (1, 1), (0, 2), (2, 0), (0, 3), (1, 2),
    (1, 3), (3, 0), (2, 1), (2, 2), (2, 3), (3, 1), (3, 2), (3, 3),
]
LAG = 2


def steps():
    at = {3: ["w0"], 8: ["w1"], 10: ["w2"], 11: ["p0"], 13: ["p1"], 15: ["b0.1"]}
    order = ["s0"]
    for s in range(len(XSEQ)):
        if s > 0:
            order.append(f"s{s}")
        if s == 0:
            order.append("w")
        if s + 1 < len(XSEQ):
            order.append(f"z{s + 1}")
        if s >= LAG:
            order.append(f"f{s - LAG}")
        order += at.get(s, [])
    order += [f"f{s}" for s in range(len(XSEQ) - LAG, len(XSEQ) - 1)]
    order += ["p2", "b1.1", "b0.2", "b0.3", "p3", "u0.0", "b1.2", "u1.0", "b1.3", "b2.1", "u0.1", "u1.1"]
    order += ["b2.2", "b3.1", "b2.3", "u0.2", "u1.2", "b3.2", "b3.3"]
    return order


def kernel(
    hidden_ref, wq_ref, wkv_ref, routing_ref, hosts_ref,
    att_ref, cache_ref,
    hid, wq, wkv, kv, acc, qbuf, sbuf, mbuf, lbuf, abuf, cbuf,
    loc_sem, z_recv, z_send, x_recv, xh_recv, x_send,
    w_recv, w_send, wy_recv, wy_send, ws_recv, ws_send,
    y_recv, y_send, s_recv, s_send, c_recv, c_send, a_sem,
):
    b = lax.axis_index("blk")
    t = lax.axis_index("tp")
    c, y, h = b % 2, (b // 2) % 4, b // 8
    x, z = t % 4, t // 4
    part = b % 8
    xr, xl, xo = (x + 1) % 4, (x + 3) % 4, (x + 2) % 4
    yr, yl, yo = (y + 1) % 4, (y + 3) % 4, (y + 2) % 4
    dev_xr, dev_xl = (b, z * 4 + xr), (b, z * 4 + xl)
    dev_y = [(h * 8 + yy * 2 + c, t) for yy in (yr, yl, yo)]
    dev_xo = (b, z * 4 + xo)
    dev_sib = (b + 1 - 2 * c, t)
    dev_far = ((1 - h) * 8 + y * 2 + c, t)

    def rcopy(src, dst, ssem, rsem, dev):
        return pltpu.make_async_remote_copy(
            src_ref=src, dst_ref=dst, send_sem=ssem, recv_sem=rsem, device_id=dev, device_id_type=MESH
        )

    def recv(ref, rsem):
        rcopy(ref, ref, x_send.at[0], rsem, dev_xr).wait_recv()

    def sent(ref, ssem):
        rcopy(ref, ref, ssem, w_recv.at[0], dev_xr).wait_send()

    own_hid = pltpu.make_async_copy(hidden_ref, hid.at[z, x], loc_sem.at[0])
    own_hid.start()
    load_wq = pltpu.make_async_copy(wq_ref, wq, loc_sem.at[1])
    load_wq.start()

    barrier = pltpu.get_barrier_semaphore()

    def greet(dev):
        pl.semaphore_signal(barrier, inc=1, device_id=dev, device_id_type=MESH)

    def greet_tp(i, carry):
        greet((b, (t + i) % NT))
        return carry

    lax.fori_loop(1, NT, greet_tp, 0)
    for dev in (*dev_y, dev_sib, dev_far):
        greet(dev)
    pl.semaphore_wait(barrier, NT - 1 + 5)

    def rows(r):
        return pl.ds(r * RC, RC)

    def half(r, i):
        return pl.ds(r * RC + i * HC, HC)

    def zk(k):
        return (z, z + 1 - 2 * (z % 2), 2 - z // 2, 3 - 3 * (z // 2))[k]

    def piece_of(s):
        r, k = XSEQ[s]
        zp = zk(k)
        return r, zp, r * 4 + zp

    def z_step(s):
        r, zp, g = piece_of(s)
        ref = hid.at[zp, x, rows(r)]
        if XSEQ[s][1] > 0:
            recv(ref, z_recv.at[g])

        @pl.when((z < 3) & (zp <= z))
        def _():
            rcopy(ref, ref, z_send.at[0, zp], z_recv.at[g], (b, t + 4)).start()

        @pl.when((z > 0) & (zp >= z))
        def _():
            rcopy(ref, ref, z_send.at[1, zp], z_recv.at[g], (b, t - 4)).start()

    def a_send(s):
        r, zp, g = piece_of(s)
        ref = hid.at[zp, x, rows(r)]
        rcopy(ref, ref, x_send.at[0], x_recv.at[0, g], dev_xr).start()
        rcopy(ref, ref, x_send.at[1], x_recv.at[1, g], dev_xl).start()
        if s == len(XSEQ) - 1:
            rcopy(ref, ref, x_send.at[2], xh_recv.at[r], dev_xo).start()

    def a_forward(s):
        r, zp, g = piece_of(s)
        recv(hid.at[zp, xl, rows(r)], x_recv.at[0, g])
        ref = hid.at[zp, xl, half(r, 0)]
        rcopy(ref, ref, x_send.at[2], xh_recv.at[r], dev_xr).start()
        recv(hid.at[zp, xr, rows(r)], x_recv.at[1, g])
        ref = hid.at[zp, xr, half(r, 1)]
        rcopy(ref, ref, x_send.at[3], xh_recv.at[r], dev_xl).start()

    def a_finish(r):
        recv(hid.at[:, xo, rows(r)], xh_recv.at[r])
        if r == R - 1:
            _, zp, g = piece_of(len(XSEQ) - 1)
            recv(hid.at[zp, xl, rows(r)], x_recv.at[0, g])
            recv(hid.at[zp, xr, rows(r)], x_recv.at[1, g])

    def a_drain():
        for kind in range(2):
            sent(hid.at[:, x], x_send.at[kind])
        sent(hid.at[pl.ds(0, 2), x], x_send.at[2])
        sent(hid.at[0, x, pl.ds(0, HC)], x_send.at[2])
        sent(hid.at[0, x], x_send.at[3])
        sent(hid.at[0, x, pl.ds(0, 3 * RC + HC)], x_send.at[3])
        for zp in range(4):
            @pl.when((z < 3) & (zp <= z))
            def _():
                sent(hid.at[zp, x], z_send.at[0, zp])

            @pl.when((z > 0) & (zp >= z))
            def _():
                sent(hid.at[zp, x], z_send.at[1, zp])

    def w_start():
        src_rows = pl.ds(part * PART, PART)

        def piece(to):
            return wkv_ref.at[src_rows, pl.ds(pl.multiple_of((to // 2) * 2 * HD, 2 * HD), 2 * HD)]

        def one(i, carry):
            to = (t + i) % NT
            rcopy(piece(to), wkv.at[t, y, c], w_send.at[0], w_recv.at[0], (b, to)).start()
            return carry

        pltpu.make_async_copy(piece(t), wkv.at[t, y, c], w_recv.at[0]).start()
        lax.fori_loop(1, NT, one, 0)

    def w_step(i):
        if i == 0:
            ref = wkv.at[:, y, c]
            recv(ref, w_recv.at[0])
            for j in range(3):
                rcopy(ref, ref, wy_send.at[0], wy_recv.at[0], dev_y[j]).start()
        elif i == 1:
            recv(wkv.at[:, pl.ds(0, 3), c], wy_recv.at[0])
            ref = wkv.at[:, :, c]
            rcopy(ref, ref, ws_send.at[0], ws_recv.at[0], dev_sib).start()
        else:
            recv(wkv.at[:, :, 1 - c], ws_recv.at[0])

    def w_drain():
        sent(wkv.at[pl.ds(0, NT - 1), y, c], w_send.at[0])
        sent(wkv.at[:, pl.ds(0, 3), c], wy_send.at[0])
        sent(wkv.at[:, :, c], ws_send.at[0])

    def project(r):
        acc[...] = jnp.zeros_like(acc)

        def body(zp, carry):
            for side in range(2):
                total = None
                for xp in range(4):
                    rhs = wq[zp * 4 + xp] if side == 0 else wkv[zp * 4 + xp].reshape(FD, 2 * HD)
                    one = jnp.dot(hid[zp, xp, rows(r)], rhs, preferred_element_type=jnp.float32)
                    total = one if total is None else total + one
                acc[side] += total
            return carry

        lax.fori_loop(0, 4, body, 0)
        kv[h, y, c, rows(r)] = acc[1].astype(jnp.bfloat16)
        for head in range(2):
            at = (r // 2) * TILE + head * (TILE // 2) + (r % 2) * RC
            qbuf[pl.ds(at, RC)] = acc[0, :, head * HD : (head + 1) * HD].astype(jnp.bfloat16)

    def b_send(r, far):
        ref = kv.at[(h + far) % 2, y, c, rows(r)]
        for j in range(3):
            rcopy(ref, ref, y_send.at[0], y_recv.at[r, far], dev_y[j]).start()

    def b_share(r, far):
        recv(kv.at[0, pl.ds(0, 3), c, rows(r)], y_recv.at[r, far])
        ref = kv.at[(h + far) % 2, :, c, rows(r)]
        rcopy(ref, ref, s_send.at[0], s_recv.at[r], dev_sib).start()

    def b_step(r, i):
        if i == 0:
            ref = kv.at[h, y, c, rows(r)]
            rcopy(ref, ref, c_send.at[0], c_recv.at[r], dev_far).start()
            b_send(r, 0)
        elif i == 1:
            recv(kv.at[1 - h, y, c, rows(r)], c_recv.at[r])
            b_send(r, 1)
            b_share(r, 0)
        elif i == 2:
            b_share(r, 1)
        else:
            recv(kv.at[:, :, 1 - c, rows(r)], s_recv.at[r])

    def b_drain():
        sent(kv.at[0, pl.ds(0, 3)], y_send.at[0])
        sent(kv.at[:, :, 0], s_send.at[0])
        sent(kv.at[0, 0, 0], c_send.at[0])

    quads = b // QUAD

    def quad_of(p, r, first):
        return kv[p // 2, pl.ds((p % 2) * 2, 2), :, rows(r), first : first + HD].reshape(QUAD * RC, HD)

    def unit(i, r):
        at = pl.ds(i * TILE, TILE)
        q = qbuf[at]
        start = jnp.full((TILE, HD), NEG, jnp.float32) if r == 0 else mbuf[i, r - 1]

        def scores(p):
            return SCALE2 * lax.dot_general(
                q, quad_of(p, r, 0), (((1,), (1,)), ((), ())), preferred_element_type=jnp.float32
            )

        def keep(p, s, m):
            sbuf[i, r, p] = s
            for j in range(QUAD):
                m = jnp.maximum(m, s[:, j * RC : (j + 1) * RC])
            return m

        m = lax.fori_loop(0, quads, lambda p, m: keep(p, scores(p), m), start)
        row = lax.broadcasted_iota(jnp.int32, (TILE, QUAD * RC), 0) % (TILE // 2) + (b * TOK + i * (TILE // 2))
        col = lax.broadcasted_iota(jnp.int32, (TILE, QUAD * RC), 1)
        col = col % RC + (col // RC) * TOK + (quads * QUAD * TOK + r * RC)
        m = keep(quads, jnp.where(col <= row, scores(quads), NEG), m)
        m = jnp.broadcast_to(jnp.max(m, axis=1, keepdims=True), (TILE, HD))
        mbuf[i, r] = m

        def exps(p, total):
            s = sbuf[i, r, p]
            e = [jnp.exp2(s[:, j * RC : (j + 1) * RC] - m) for j in range(QUAD)]
            sbuf[i, r, p] = jnp.concatenate(e, axis=1)
            return total + ((e[0] + e[1]) + (e[2] + e[3]))

        total = jnp.zeros((TILE, HD), jnp.float32) if r == 0 else lbuf[i] * jnp.exp2(start - m)
        lbuf[i] = lax.fori_loop(0, quads + 1, exps, total)

    def values(i):
        final = mbuf[i, R - 1]
        out = jnp.zeros((TILE, HD), jnp.float32)
        for r in range(R):
            factor = None if r == R - 1 else jnp.exp2(mbuf[i, r] - final)

            def body(p, out):
                e = sbuf[i, r, p]
                if factor is not None:
                    e = jnp.concatenate([e[:, j * RC : (j + 1) * RC] * factor for j in range(QUAD)], axis=1)
                return out + jnp.dot(
                    e.astype(jnp.bfloat16), quad_of(p, r, HD), preferred_element_type=jnp.float32
                )

            out = lax.fori_loop(0, quads + 1, body, out)
        out = (out / jnp.sum(lbuf[i], axis=1, keepdims=True)).astype(jnp.bfloat16)
        at = pl.ds(i * (TILE // 2), TILE // 2)
        abuf[at, 0:HD] = out[: TILE // 2]
        abuf[at, HD:] = out[TILE // 2 :]
        pltpu.make_async_copy(abuf.at[at], att_ref.at[at], a_sem.at[0]).start()

    own_hid.wait()
    for step in steps():
        what, number = step[0], step[1:]
        if what == "s":
            if XSEQ[int(number)][1] == 0:
                z_step(int(number))
            a_send(int(number))
        elif what == "z":
            if XSEQ[int(number)][1] > 0:
                z_step(int(number))
        elif what == "f":
            a_forward(int(number))
        elif what == "w":
            w_step(int(number)) if number else w_start()
        elif what == "p":
            r = int(number)
            if r == 0:
                load_wq.wait()
            a_finish(r)
            project(r)
            b_step(r, 0)
        elif what == "b":
            b_step(int(number[0]), int(number[2]))
        else:
            unit(int(number[0]), int(number[2]))
    for i in range(2):
        unit(i, R - 1)

    count = jnp.int32(0)
    index = [jnp.int32(0)] * CAP
    for bb in range(NB):
        hit = hosts_ref[routing_ref[bb]] == b
        for s in range(CAP):
            index[s] = jnp.where(hit & (count == s), bb, index[s])
        count = count + hit.astype(jnp.int32)
    for s in range(CAP):
        @pl.when(t % 2 == 0)
        def _():
            cbuf[s] = jnp.where(s < count, kv[index[s] // 8, (index[s] // 2) % 4, index[s] % 2, :, 0:HD], jnp.zeros((TOK, HD), jnp.bfloat16))

        @pl.when(t % 2 == 1)
        def _():
            cbuf[s] = jnp.where(s < count, kv[index[s] // 8, (index[s] // 2) % 4, index[s] % 2, :, HD:], jnp.zeros((TOK, HD), jnp.bfloat16))
    store_cache = pltpu.make_async_copy(cbuf, cache_ref, loc_sem.at[2])
    store_cache.start()

    for i in range(2):
        values(i)

    a_drain()
    w_drain()
    b_drain()
    store_cache.wait()
    pltpu.make_async_copy(abuf, att_ref, a_sem.at[0]).wait()


def local(hidden_in, w_query, w_keyval, routing, hosts):
    any_spec = pl.BlockSpec(memory_space=pl.ANY)
    smem = pl.BlockSpec(memory_space=pltpu.SMEM)
    dma = pltpu.SemaphoreType.DMA
    bf16, f32 = jnp.bfloat16, jnp.float32
    attended, cache = pl.pallas_call(
        kernel,
        out_shape=(
            jax.ShapeDtypeStruct((TOK, 2 * HD), bf16),
            jax.ShapeDtypeStruct((CAP, TOK, HD), bf16),
        ),
        in_specs=[any_spec, any_spec, any_spec, smem, smem],
        out_specs=(any_spec, any_spec),
        scratch_shapes=[
            pltpu.VMEM((4, 4, TOK, FD), bf16),
            pltpu.VMEM((NT, FD, 2 * HD), bf16),
            pltpu.VMEM((NT, 4, 2, PART, 2 * HD), bf16),
            pltpu.VMEM((2, 4, 2, TOK, 2 * HD), bf16),
            pltpu.VMEM((2, RC, 2 * HD), f32),
            pltpu.VMEM((2 * TILE, HD), bf16),
            pltpu.VMEM((2, R, NB // QUAD, TILE, QUAD * RC), f32),
            pltpu.VMEM((2, R, TILE, HD), f32),
            pltpu.VMEM((2, TILE, HD), f32),
            pltpu.VMEM((TOK, 2 * HD), bf16),
            pltpu.VMEM((CAP, TOK, HD), bf16),
            dma((3,)),
            dma((4 * R,)), dma((2, 4)),
            dma((2, 4 * R)), dma((R,)), dma((4,)),
            dma((1,)), dma((1,)),
            dma((1,)), dma((1,)),
            dma((1,)), dma((1,)),
            dma((R, 2)), dma((1,)),
            dma((R,)), dma((1,)),
            dma((R,)), dma((1,)),
            dma((1,)),
        ],
        compiler_params=pltpu.CompilerParams(
            collective_id=0, has_side_effects=True, vmem_limit_bytes=58 * 1024 * 1024
        ),
        cost_estimate=pl.CostEstimate(flops=8 * 10**9, bytes_accessed=8 * 2**20, transcendentals=8 * 2**20),
    )(hidden_in, w_query.reshape(NT, FD, 2 * HD), w_keyval, routing.reshape(NB), hosts)
    return attended, cache[None]


def solution(mesh):
    in_specs = (P("blk", "tp"), P(None, "tp"), P("tp", None), P(), P())
    out_specs = (P("blk", "tp"), P("blk", None, None, "tp"))
    return jax.shard_map(local, mesh=mesh, in_specs=in_specs, out_specs=out_specs, check_vma=False)
```

```python
import functools

import jax
import jax.numpy as jnp
from jax import lax
from jax.experimental import pallas as pl
from jax.experimental.pallas import tpu as pltpu
from jax.sharding import PartitionSpec as P

HEADS = 32
KVH = 8
HD = 128
TOK = 512
CAP = 8
NB = 16
NT = 16
FD = 256
PART = 32
R = 4
RC = TOK // R
HC = RC // 2
TILE = 2 * TOK // 2
QUAD = 4
MESH = pl.DeviceIdType.MESH
LOG2E = 1.4426950408889634
SCALE2 = HD**-0.5 * LOG2E
NEG = -1e30

XSEQ = [
    (0, 0), (1, 0), (0, 1), (1, 1), (0, 2), (2, 0), (0, 3), (1, 2),
    (1, 3), (3, 0), (2, 1), (2, 2), (2, 3), (3, 1), (3, 2), (3, 3),
]
LAG = 2


def steps():
    at = {3: ["w0"], 8: ["w1"], 10: ["w2"], 11: ["p0"], 13: ["p1"], 15: ["b0.1"]}
    order = ["s0"]
    for s in range(len(XSEQ)):
        if s > 0:
            order.append(f"s{s}")
        if s == 0:
            order.append("w")
        if s + 1 < len(XSEQ):
            order.append(f"z{s + 1}")
        if s >= LAG:
            order.append(f"f{s - LAG}")
        order += at.get(s, [])
    order += [f"f{s}" for s in range(len(XSEQ) - LAG, len(XSEQ) - 1)]
    order += ["p2", "b1.1", "b0.2", "b0.3", "p3", "u0.0", "b1.2", "u1.0", "b1.3", "b2.1", "u0.1", "u1.1"]
    order += ["b2.2", "b3.1k", "b3.1v", "b2.3", "u0.2", "u1.2", "b3.2k", "b3.2v", "b3.3k", "u0.3", "u1.3", "b3.3v"]
    return order


def kernel(
    hidden_ref, wq_ref, wkv_ref, routing_ref, hosts_ref,
    att_ref, cache_ref,
    hid, wq, wkv, kv, acc, qbuf, sbuf, mbuf, lbuf, abuf, cbuf,
    loc_sem, z_recv, z_send, x_recv, xh_recv, x_send,
    w_recv, w_send, wy_recv, wy_send, ws_recv, ws_send,
    y_recv, y_send, s_recv, s_send, c_recv, c_send, a_sem,
):
    b = lax.axis_index("blk")
    t = lax.axis_index("tp")
    c, y, h = b % 2, (b // 2) % 4, b // 8
    x, z = t % 4, t // 4
    part = b % 8
    xr, xl, xo = (x + 1) % 4, (x + 3) % 4, (x + 2) % 4
    yr, yl, yo = (y + 1) % 4, (y + 3) % 4, (y + 2) % 4
    dev_xr, dev_xl = (b, z * 4 + xr), (b, z * 4 + xl)
    dev_y = [(h * 8 + yy * 2 + c, t) for yy in (yr, yl, yo)]
    dev_xo = (b, z * 4 + xo)
    dev_sib = (b + 1 - 2 * c, t)
    dev_far = ((1 - h) * 8 + y * 2 + c, t)

    def rcopy(src, dst, ssem, rsem, dev):
        return pltpu.make_async_remote_copy(
            src_ref=src, dst_ref=dst, send_sem=ssem, recv_sem=rsem, device_id=dev, device_id_type=MESH
        )

    def recv(ref, rsem):
        rcopy(ref, ref, x_send.at[0], rsem, dev_xr).wait_recv()

    def sent(ref, ssem):
        rcopy(ref, ref, ssem, w_recv.at[0], dev_xr).wait_send()

    own_hid = pltpu.make_async_copy(hidden_ref, hid.at[z, x], loc_sem.at[0])
    own_hid.start()
    load_wq = pltpu.make_async_copy(wq_ref, wq, loc_sem.at[1])
    load_wq.start()

    barrier = pltpu.get_barrier_semaphore()

    def greet(dev):
        pl.semaphore_signal(barrier, inc=1, device_id=dev, device_id_type=MESH)

    def greet_tp(i, carry):
        greet((b, (t + i) % NT))
        return carry

    lax.fori_loop(1, NT, greet_tp, 0)
    for dev in (*dev_y, dev_sib, dev_far):
        greet(dev)
    pl.semaphore_wait(barrier, NT - 1 + 5)

    def rows(r):
        return pl.ds(r * RC, RC)

    def half(r, i):
        return pl.ds(r * RC + i * HC, HC)

    def zk(k):
        return (z, z + 1 - 2 * (z % 2), 2 - z // 2, 3 - 3 * (z // 2))[k]

    def piece_of(s):
        r, k = XSEQ[s]
        zp = zk(k)
        return r, zp, r * 4 + zp

    def z_step(s):
        r, zp, g = piece_of(s)
        ref = hid.at[zp, x, rows(r)]
        if XSEQ[s][1] > 0:
            recv(ref, z_recv.at[g])

        @pl.when((z < 3) & (zp <= z))
        def _():
            rcopy(ref, ref, z_send.at[0, zp], z_recv.at[g], (b, t + 4)).start()

        @pl.when((z > 0) & (zp >= z))
        def _():
            rcopy(ref, ref, z_send.at[1, zp], z_recv.at[g], (b, t - 4)).start()

    def a_send(s):
        r, zp, g = piece_of(s)
        ref = hid.at[zp, x, rows(r)]
        rcopy(ref, ref, x_send.at[0], x_recv.at[0, g], dev_xr).start()
        rcopy(ref, ref, x_send.at[1], x_recv.at[1, g], dev_xl).start()
        if s == len(XSEQ) - 1:
            rcopy(ref, ref, x_send.at[2], xh_recv.at[r], dev_xo).start()

    def a_forward(s):
        r, zp, g = piece_of(s)
        recv(hid.at[zp, xl, rows(r)], x_recv.at[0, g])
        ref = hid.at[zp, xl, half(r, 0)]
        rcopy(ref, ref, x_send.at[2], xh_recv.at[r], dev_xr).start()
        recv(hid.at[zp, xr, rows(r)], x_recv.at[1, g])
        ref = hid.at[zp, xr, half(r, 1)]
        rcopy(ref, ref, x_send.at[3], xh_recv.at[r], dev_xl).start()

    def a_finish(r):
        recv(hid.at[:, xo, rows(r)], xh_recv.at[r])
        if r == R - 1:
            _, zp, g = piece_of(len(XSEQ) - 1)
            recv(hid.at[zp, xl, rows(r)], x_recv.at[0, g])
            recv(hid.at[zp, xr, rows(r)], x_recv.at[1, g])

    def a_drain():
        for kind in range(2):
            sent(hid.at[:, x], x_send.at[kind])
        sent(hid.at[pl.ds(0, 2), x], x_send.at[2])
        sent(hid.at[0, x, pl.ds(0, HC)], x_send.at[2])
        sent(hid.at[0, x], x_send.at[3])
        sent(hid.at[0, x, pl.ds(0, 3 * RC + HC)], x_send.at[3])
        for zp in range(4):
            @pl.when((z < 3) & (zp <= z))
            def _():
                sent(hid.at[zp, x], z_send.at[0, zp])

            @pl.when((z > 0) & (zp >= z))
            def _():
                sent(hid.at[zp, x], z_send.at[1, zp])

    def w_start():
        src_rows = pl.ds(part * PART, PART)

        def piece(to):
            return wkv_ref.at[src_rows, pl.ds(pl.multiple_of((to // 2) * 2 * HD, 2 * HD), 2 * HD)]

        def one(i, carry):
            to = (t + i) % NT
            rcopy(piece(to), wkv.at[t, y, c], w_send.at[0], w_recv.at[0], (b, to)).start()
            return carry

        pltpu.make_async_copy(piece(t), wkv.at[t, y, c], w_recv.at[0]).start()
        lax.fori_loop(1, NT, one, 0)

    def w_step(i):
        if i == 0:
            ref = wkv.at[:, y, c]
            recv(ref, w_recv.at[0])
            for j in range(3):
                rcopy(ref, ref, wy_send.at[0], wy_recv.at[0], dev_y[j]).start()
        elif i == 1:
            recv(wkv.at[:, pl.ds(0, 3), c], wy_recv.at[0])
            ref = wkv.at[:, :, c]
            rcopy(ref, ref, ws_send.at[0], ws_recv.at[0], dev_sib).start()
        else:
            recv(wkv.at[:, :, 1 - c], ws_recv.at[0])

    def w_drain():
        sent(wkv.at[pl.ds(0, NT - 1), y, c], w_send.at[0])
        sent(wkv.at[:, pl.ds(0, 3), c], wy_send.at[0])
        sent(wkv.at[:, :, c], ws_send.at[0])

    def project(r):
        acc[...] = jnp.zeros_like(acc)

        def body(zp, carry):
            for side in range(2):
                total = None
                for xp in range(4):
                    rhs = wq[zp * 4 + xp] if side == 0 else wkv[zp * 4 + xp].reshape(FD, 2 * HD)
                    one = jnp.dot(hid[zp, xp, rows(r)], rhs, preferred_element_type=jnp.float32)
                    total = one if total is None else total + one
                acc[side] += total
            return carry

        lax.fori_loop(0, 4, body, 0)
        for j in range(2):
            kv[j, h, y, c, rows(r)] = acc[1, :, j * HD : (j + 1) * HD].astype(jnp.bfloat16)
        for head in range(2):
            at = (r // 2) * TILE + head * (TILE // 2) + (r % 2) * RC
            qbuf[pl.ds(at, RC)] = acc[0, :, head * HD : (head + 1) * HD].astype(jnp.bfloat16)

    def sides(part):
        return pl.ds(0, 2) if part == 2 else pl.ds(part, 1)

    def slot(r, part):
        return R if part == 1 else r

    def b_send(r, part, far):
        ref = kv.at[sides(part), (h + far) % 2, y, c, rows(r)]
        for j in range(3):
            rcopy(ref, ref, y_send.at[0], y_recv.at[slot(r, part), far], dev_y[j]).start()

    def b_share(r, part, far):
        hh = (h + far) % 2
        recv(kv.at[sides(part), hh, pl.ds(0, 3), c, rows(r)], y_recv.at[slot(r, part), far])
        ref = kv.at[sides(part), hh, :, c, rows(r)]
        rcopy(ref, ref, s_send.at[0], s_recv.at[slot(r, part)], dev_sib).start()

    def b_step(r, i, part=2):
        at = slot(r, part)
        if i == 0:
            ref = kv.at[sides(part), h, y, c, rows(r)]
            rcopy(ref, ref, c_send.at[0], c_recv.at[at], dev_far).start()
            b_send(r, part, 0)
        elif i == 1:
            recv(kv.at[sides(part), 1 - h, y, c, rows(r)], c_recv.at[at])
            b_send(r, part, 1)
            b_share(r, part, 0)
        elif i == 2:
            b_share(r, part, 1)
        else:
            recv(kv.at[sides(part), :, :, 1 - c, rows(r)], s_recv.at[at])

    def b_drain():
        sent(kv.at[:, 0, pl.ds(0, 3)], y_send.at[0])
        sent(kv.at[:, :, :, 0], s_send.at[0])
        sent(kv.at[:, 0, 0, 0], c_send.at[0])

    quads = b // QUAD

    def quad_of(p, r, first):
        return kv[first, p // 2, pl.ds((p % 2) * 2, 2), :, rows(r)].reshape(QUAD * RC, HD)

    def unit(i, r):
        at = pl.ds(i * TILE, TILE)
        q = qbuf[at]
        start = jnp.full((TILE, HD), NEG, jnp.float32) if r == 0 else mbuf[i, r - 1]

        def scores(p):
            return SCALE2 * lax.dot_general(
                q, quad_of(p, r, 0), (((1,), (1,)), ((), ())), preferred_element_type=jnp.float32
            )

        def keep(p, s, m):
            sbuf[i, r, p] = s
            for j in range(QUAD):
                m = jnp.maximum(m, s[:, j * RC : (j + 1) * RC])
            return m

        m = lax.fori_loop(0, quads, lambda p, m: keep(p, scores(p), m), start)
        row = lax.broadcasted_iota(jnp.int32, (TILE, QUAD * RC), 0) % (TILE // 2) + (b * TOK + i * (TILE // 2))
        col = lax.broadcasted_iota(jnp.int32, (TILE, QUAD * RC), 1)
        col = col % RC + (col // RC) * TOK + (quads * QUAD * TOK + r * RC)
        m = keep(quads, jnp.where(col <= row, scores(quads), NEG), m)
        m = jnp.broadcast_to(jnp.max(m, axis=1, keepdims=True), (TILE, HD))
        mbuf[i, r] = m

        def exps(p, total):
            s = sbuf[i, r, p]
            e = [jnp.exp2(s[:, j * RC : (j + 1) * RC] - m) for j in range(QUAD)]
            sbuf[i, r, p] = jnp.concatenate(e, axis=1)
            return total + ((e[0] + e[1]) + (e[2] + e[3]))

        total = jnp.zeros((TILE, HD), jnp.float32) if r == 0 else lbuf[i] * jnp.exp2(start - m)
        lbuf[i] = lax.fori_loop(0, quads + 1, exps, total)

    def values(i):
        final = mbuf[i, R - 1]
        for r in range(R - 1):
            mbuf[i, r] = jnp.exp2(mbuf[i, r] - final)

        def body(p, out):
            for r in range(R):
                e = sbuf[i, r, p]
                if r < R - 1:
                    e = jnp.concatenate([e[:, j * RC : (j + 1) * RC] * mbuf[i, r] for j in range(QUAD)], axis=1)
                out = out + jnp.dot(
                    e.astype(jnp.bfloat16), quad_of(p, r, 1), preferred_element_type=jnp.float32
                )
            return out

        out = lax.fori_loop(0, quads + 1, body, jnp.zeros((TILE, HD), jnp.float32))
        out = (out / jnp.sum(lbuf[i], axis=1, keepdims=True)).astype(jnp.bfloat16)
        at = pl.ds(i * (TILE // 2), TILE // 2)
        abuf[at, 0:HD] = out[: TILE // 2]
        abuf[at, HD:] = out[TILE // 2 :]
        pltpu.make_async_copy(abuf.at[at], att_ref.at[at], a_sem.at[0]).start()

    own_hid.wait()
    for step in steps():
        what, number = step[0], step[1:]
        if what == "s":
            if XSEQ[int(number)][1] == 0:
                z_step(int(number))
            a_send(int(number))
        elif what == "z":
            if XSEQ[int(number)][1] > 0:
                z_step(int(number))
        elif what == "f":
            a_forward(int(number))
        elif what == "w":
            w_step(int(number)) if number else w_start()
        elif what == "p":
            r = int(number)
            if r == 0:
                load_wq.wait()
            a_finish(r)
            project(r)
            if r < R - 1:
                b_step(r, 0)
            else:
                b_step(r, 0, 0)
                b_step(r, 0, 1)
        elif what == "b":
            b_step(int(number[0]), int(number[2]), "kv".find(number[3:]) if number[3:] else 2)
        else:
            unit(int(number[0]), int(number[2]))

    count = jnp.int32(0)
    index = [jnp.int32(0)] * CAP
    for bb in range(NB):
        hit = hosts_ref[routing_ref[bb]] == b
        for s in range(CAP):
            index[s] = jnp.where(hit & (count == s), bb, index[s])
        count = count + hit.astype(jnp.int32)
    for s in range(CAP):
        mine = kv[t % 2, index[s] // 8, (index[s] // 2) % 4, index[s] % 2]
        cbuf[s] = jnp.where(s < count, mine, jnp.zeros((TOK, HD), jnp.bfloat16))
    store_cache = pltpu.make_async_copy(cbuf, cache_ref, loc_sem.at[2])
    store_cache.start()

    for i in range(2):
        values(i)

    a_drain()
    w_drain()
    b_drain()
    store_cache.wait()
    pltpu.make_async_copy(abuf, att_ref, a_sem.at[0]).wait()


def local(hidden_in, w_query, w_keyval, routing, hosts):
    any_spec = pl.BlockSpec(memory_space=pl.ANY)
    smem = pl.BlockSpec(memory_space=pltpu.SMEM)
    dma = pltpu.SemaphoreType.DMA
    bf16, f32 = jnp.bfloat16, jnp.float32
    attended, cache = pl.pallas_call(
        kernel,
        out_shape=(
            jax.ShapeDtypeStruct((TOK, 2 * HD), bf16),
            jax.ShapeDtypeStruct((CAP, TOK, HD), bf16),
        ),
        in_specs=[any_spec, any_spec, any_spec, smem, smem],
        out_specs=(any_spec, any_spec),
        scratch_shapes=[
            pltpu.VMEM((4, 4, TOK, FD), bf16),
            pltpu.VMEM((NT, FD, 2 * HD), bf16),
            pltpu.VMEM((NT, 4, 2, PART, 2 * HD), bf16),
            pltpu.VMEM((2, 2, 4, 2, TOK, HD), bf16),
            pltpu.VMEM((2, RC, 2 * HD), f32),
            pltpu.VMEM((2 * TILE, HD), bf16),
            pltpu.VMEM((2, R, NB // QUAD, TILE, QUAD * RC), f32),
            pltpu.VMEM((2, R, TILE, HD), f32),
            pltpu.VMEM((2, TILE, HD), f32),
            pltpu.VMEM((TOK, 2 * HD), bf16),
            pltpu.VMEM((CAP, TOK, HD), bf16),
            dma((3,)),
            dma((4 * R,)), dma((2, 4)),
            dma((2, 4 * R)), dma((R,)), dma((4,)),
            dma((1,)), dma((1,)),
            dma((1,)), dma((1,)),
            dma((1,)), dma((1,)),
            dma((R + 1, 2)), dma((1,)),
            dma((R + 1,)), dma((1,)),
            dma((R + 1,)), dma((1,)),
            dma((1,)),
        ],
        compiler_params=pltpu.CompilerParams(
            collective_id=0, has_side_effects=True, vmem_limit_bytes=58 * 1024 * 1024
        ),
        cost_estimate=pl.CostEstimate(flops=8 * 10**9, bytes_accessed=8 * 2**20, transcendentals=8 * 2**20),
    )(hidden_in, w_query.reshape(NT, FD, 2 * HD), w_keyval, routing.reshape(NB), hosts)
    return attended, cache[None]


def solution(mesh):
    in_specs = (P("blk", "tp"), P(None, "tp"), P("tp", None), P(), P())
    out_specs = (P("blk", "tp"), P("blk", None, None, "tp"))
    return jax.shard_map(local, mesh=mesh, in_specs=in_specs, out_specs=out_specs, check_vma=False)
```

```python
import functools

import jax
import jax.numpy as jnp
from jax import lax
from jax.experimental import pallas as pl
from jax.experimental.pallas import tpu as pltpu
from jax.sharding import PartitionSpec as P

HEADS = 32
KVH = 8
HD = 128
TOK = 512
CAP = 8
NB = 16
NT = 16
FD = 256
PART = 32
R = 4
RC = TOK // R
HC = RC // 2
TILE = 2 * TOK // 2
QUAD = 4
MESH = pl.DeviceIdType.MESH
LOG2E = 1.4426950408889634
SCALE2 = HD**-0.5 * LOG2E
NEG = -1e30

XSEQ = [
    (0, 0), (1, 0), (0, 1), (1, 1), (0, 2), (2, 0), (0, 3), (1, 2),
    (1, 3), (3, 0), (2, 1), (2, 2), (2, 3), (3, 1), (3, 2), (3, 3),
]
LAG = 2


def steps():
    at = {
        0: ["wa", "wb", "wc"], 3: ["w0"], 9: ["w1"], 11: ["w2", "p0"], 13: ["p1"], 15: ["b0.1", "b0.n", "p2"],
    }
    order = ["s0"]
    for s in range(len(XSEQ)):
        if s > 0:
            order.append(f"s{s}")
        if s + 1 < len(XSEQ):
            order.append(f"z{s + 1}")
        if s >= LAG:
            order.append(f"f{s - LAG}")
        order += at.get(s, [])
    order += [f"f{s}" for s in range(len(XSEQ) - LAG, len(XSEQ) - 1)]
    order += ["b1.n", "b1.1", "b0.f", "b0.N", "b0.F", "un00", "uf00", "q3", "p3", "b2.n", "b2.1", "un01"]
    order += ["uf01", "b1.f", "b3.nk", "b1.N", "b3.nv", "un10", "b3.1k", "b3.1v", "b1.F", "un11", "uf10", "uf11"]
    order += ["b2.f", "b2.N", "b2.F", "un20", "un21", "b3.fk", "b3.fv", "b3.Nk", "un30", "un31", "b3.Nv", "b3.Fk"]
    order += ["uf20", "uf21", "uf30", "uf31", "b3.Fv"]
    return order


def kernel(
    hidden_ref, wq_ref, wkv_ref, routing_ref, hosts_ref,
    att_ref, cache_ref,
    hid, wq, wkv, kv, acc, qbuf, sbuf, mbuf, top, lbuf, abuf, cbuf,
    loc_sem, z_recv, z_send, x_recv, xh_recv, x_send,
    w_recv, w_send, wy_recv, wy_send, ws_recv, ws_send,
    y_recv, y_send, s_recv, s_send, c_recv, c_send, a_sem,
):
    b = lax.axis_index("blk")
    t = lax.axis_index("tp")
    c, y, h = b % 2, (b // 2) % 4, b // 8
    x, z = t % 4, t // 4
    part = b % 8
    xr, xl, xo = (x + 1) % 4, (x + 3) % 4, (x + 2) % 4
    yr, yl, yo = (y + 1) % 4, (y + 3) % 4, (y + 2) % 4
    dev_xr, dev_xl = (b, z * 4 + xr), (b, z * 4 + xl)
    dev_y = [(h * 8 + yy * 2 + c, t) for yy in (yr, yl, yo)]
    dev_xo = (b, z * 4 + xo)
    dev_sib = (b + 1 - 2 * c, t)
    dev_far = ((1 - h) * 8 + y * 2 + c, t)

    def rcopy(src, dst, ssem, rsem, dev):
        return pltpu.make_async_remote_copy(
            src_ref=src, dst_ref=dst, send_sem=ssem, recv_sem=rsem, device_id=dev, device_id_type=MESH
        )

    def recv(ref, rsem):
        rcopy(ref, ref, x_send.at[0], rsem, dev_xr).wait_recv()

    def sent(ref, ssem):
        rcopy(ref, ref, ssem, w_recv.at[0], dev_xr).wait_send()

    own_hid = pltpu.make_async_copy(hidden_ref, hid.at[z, x], loc_sem.at[0])
    own_hid.start()
    load_wq = pltpu.make_async_copy(wq_ref, wq, loc_sem.at[1])
    load_wq.start()

    top[...] = jnp.full(top.shape, NEG, jnp.float32)
    lbuf[...] = jnp.zeros_like(lbuf)

    barrier = pltpu.get_barrier_semaphore()

    def greet(dev):
        pl.semaphore_signal(barrier, inc=1, device_id=dev, device_id_type=MESH)

    def greet_tp(i, carry):
        greet((b, (t + i) % NT))
        return carry

    lax.fori_loop(1, NT, greet_tp, 0)
    for dev in (*dev_y, dev_sib, dev_far):
        greet(dev)
    pl.semaphore_wait(barrier, NT - 1 + 5)

    def rows(r):
        return pl.ds(r * RC, RC)

    def half(r, i):
        return pl.ds(r * RC + i * HC, HC)

    def zk(k):
        return (z, z + 1 - 2 * (z % 2), 2 - z // 2, 3 - 3 * (z // 2))[k]

    def piece_of(s):
        r, k = XSEQ[s]
        zp = zk(k)
        return r, zp, r * 4 + zp

    def z_step(s):
        r, zp, g = piece_of(s)
        ref = hid.at[zp, x, rows(r)]
        if XSEQ[s][1] > 0:
            recv(ref, z_recv.at[g])

        @pl.when((z < 3) & (zp <= z))
        def _():
            rcopy(ref, ref, z_send.at[0, zp], z_recv.at[g], (b, t + 4)).start()

        @pl.when((z > 0) & (zp >= z))
        def _():
            rcopy(ref, ref, z_send.at[1, zp], z_recv.at[g], (b, t - 4)).start()

    def a_send(s):
        r, zp, g = piece_of(s)
        ref = hid.at[zp, x, rows(r)]
        rcopy(ref, ref, x_send.at[0], x_recv.at[0, g], dev_xr).start()
        rcopy(ref, ref, x_send.at[1], x_recv.at[1, g], dev_xl).start()
        if s == len(XSEQ) - 1:
            rcopy(ref, ref, x_send.at[2], xh_recv.at[xh_of(s)], dev_xo).start()

    def xh_of(s):
        r, k = XSEQ[s]
        return r + k if r == R - 1 else r

    def a_forward(s):
        r, zp, g = piece_of(s)
        recv(hid.at[zp, xl, rows(r)], x_recv.at[0, g])
        ref = hid.at[zp, xl, half(r, 0)]
        rcopy(ref, ref, x_send.at[2], xh_recv.at[xh_of(s)], dev_xr).start()
        recv(hid.at[zp, xr, rows(r)], x_recv.at[1, g])
        ref = hid.at[zp, xr, half(r, 1)]
        rcopy(ref, ref, x_send.at[3], xh_recv.at[xh_of(s)], dev_xl).start()

    def a_finish(r):
        recv(hid.at[:, xo, rows(r)], xh_recv.at[r])

    def a_finish_last(k):
        recv(hid.at[zk(k), xo, rows(R - 1)], xh_recv.at[R - 1 + k])
        if k == 3:
            _, zp, g = piece_of(len(XSEQ) - 1)
            recv(hid.at[zp, xl, rows(R - 1)], x_recv.at[0, g])
            recv(hid.at[zp, xr, rows(R - 1)], x_recv.at[1, g])

    def a_drain():
        for kind in range(2):
            sent(hid.at[:, x], x_send.at[kind])
        sent(hid.at[pl.ds(0, 2), x], x_send.at[2])
        sent(hid.at[0, x, pl.ds(0, HC)], x_send.at[2])
        sent(hid.at[0, x], x_send.at[3])
        sent(hid.at[0, x, pl.ds(0, 3 * RC + HC)], x_send.at[3])
        for zp in range(4):
            @pl.when((z < 3) & (zp <= z))
            def _():
                sent(hid.at[zp, x], z_send.at[0, zp])

            @pl.when((z > 0) & (zp >= z))
            def _():
                sent(hid.at[zp, x], z_send.at[1, zp])

    def w_start(part_of):
        src_rows = pl.ds(part * PART, PART)

        def piece(to):
            return wkv_ref.at[src_rows, pl.ds(pl.multiple_of((to // 2) * 2 * HD, 2 * HD), 2 * HD)]

        def one(i, carry):
            to = (t + i) % NT
            rcopy(piece(to), wkv.at[t, y, c], w_send.at[0], w_recv.at[0], (b, to)).start()
            return carry

        if part_of == 0:
            pltpu.make_async_copy(piece(t), wkv.at[t, y, c], w_recv.at[0]).start()
        lax.fori_loop(1 + 5 * part_of, 6 + 5 * part_of, one, 0)

    def w_step(i):
        if i == 0:
            ref = wkv.at[:, y, c]
            recv(ref, w_recv.at[0])
            for j in range(3):
                rcopy(ref, ref, wy_send.at[0], wy_recv.at[0], dev_y[j]).start()
        elif i == 1:
            recv(wkv.at[:, pl.ds(0, 3), c], wy_recv.at[0])
            ref = wkv.at[:, :, c]
            rcopy(ref, ref, ws_send.at[0], ws_recv.at[0], dev_sib).start()
        else:
            recv(wkv.at[:, :, 1 - c], ws_recv.at[0])

    def w_drain():
        sent(wkv.at[pl.ds(0, NT - 1), y, c], w_send.at[0])
        sent(wkv.at[:, pl.ds(0, 3), c], wy_send.at[0])
        sent(wkv.at[:, :, c], ws_send.at[0])

    def product(r, zp, side):
        total = None
        for xp in range(4):
            rhs = wq[zp * 4 + xp] if side == 0 else wkv[zp * 4 + xp].reshape(FD, 2 * HD)
            one = jnp.dot(hid[zp, xp, rows(r)], rhs, preferred_element_type=jnp.float32)
            total = one if total is None else total + one
        return total

    def keep_keyval(r, total):
        for j in range(2):
            kv[j, h, y, c, rows(r)] = total[:, j * HD : (j + 1) * HD].astype(jnp.bfloat16)

    def keep_query(r, total):
        for head in range(2):
            at = (r // 2) * TILE + head * (TILE // 2) + (r % 2) * RC
            qbuf[pl.ds(at, RC)] = total[:, head * HD : (head + 1) * HD].astype(jnp.bfloat16)

    def project(r):
        acc[...] = jnp.zeros_like(acc)

        def body(zp, carry):
            for side in range(2):
                acc[side] += product(r, zp, side)
            return carry

        lax.fori_loop(0, 4, body, 0)
        keep_keyval(r, acc[1])
        keep_query(r, acc[0])

    def project_last(part):
        r = R - 1
        if part == 0:
            for side in range(2):
                acc[side] = product(r, zk(0), side) + product(r, zk(1), side)
        elif part == 1:
            keep_keyval(r, acc[1] + product(r, zk(2), 1) + product(r, zk(3), 1))
        else:
            keep_query(r, acc[0] + product(r, zk(2), 0) + product(r, zk(3), 0))

    def sides(part):
        return pl.ds(0, 2) if part == 2 else pl.ds(part, 1)

    def slot(r, part):
        return R if part == 1 else r

    def b_send(r, part, far):
        ref = kv.at[sides(part), (h + far) % 2, y, c, rows(r)]
        for j in range(3):
            rcopy(ref, ref, y_send.at[0], y_recv.at[slot(r, part), far], dev_y[j]).start()

    def b_share(r, part, far):
        hh = (h + far) % 2
        recv(kv.at[sides(part), hh, pl.ds(0, 3), c, rows(r)], y_recv.at[slot(r, part), far])
        ref = kv.at[sides(part), hh, :, c, rows(r)]
        rcopy(ref, ref, s_send.at[0], s_recv.at[slot(r, part), far], dev_sib).start()

    def b_step(r, what, part=2):
        at = slot(r, part)
        if what == "0":
            ref = kv.at[sides(part), h, y, c, rows(r)]
            rcopy(ref, ref, c_send.at[0], c_recv.at[at], dev_far).start()
            b_send(r, part, 0)
        elif what == "1":
            recv(kv.at[sides(part), 1 - h, y, c, rows(r)], c_recv.at[at])
            b_send(r, part, 1)
        elif what in "nf":
            b_share(r, part, "nf".index(what))
        else:
            far = "NF".index(what)
            recv(kv.at[sides(part), (h + far) % 2, :, 1 - c, rows(r)], s_recv.at[at, far])

    def b_drain():
        sent(kv.at[:, 0, pl.ds(0, 3)], y_send.at[0])
        sent(kv.at[:, :, :, 0], s_send.at[0])
        sent(kv.at[:, 0, 0, 0], c_send.at[0])

    quads = b // QUAD

    def quad_of(p, r, first):
        return kv[first, p // 2, pl.ds((p % 2) * 2, 2), :, rows(r)].reshape(QUAD * RC, HD)

    def unit(i, r, far):
        q = qbuf[pl.ds(i * TILE, TILE)]

        def scores(p):
            return SCALE2 * lax.dot_general(
                q, quad_of(p, r, 0), (((1,), (1,)), ((), ())), preferred_element_type=jnp.float32
            )

        def keep(p, s):
            s = [s[:, j * RC : (j + 1) * RC] for j in range(QUAD)]
            m = jnp.maximum(jnp.maximum(s[0], s[1]), jnp.maximum(s[2], s[3]))
            m = jnp.broadcast_to(jnp.max(m, axis=1, keepdims=True), (TILE, HD))
            mbuf[i, r, p] = m
            e = [jnp.exp2(one - m) for one in s]
            sbuf[i, r, p] = jnp.concatenate(e, axis=1)
            old = top[i]
            new = jnp.maximum(old, m)
            lbuf[i] = lbuf[i] * jnp.exp2(old - new) + ((e[0] + e[1]) + (e[2] + e[3])) * jnp.exp2(m - new)
            top[i] = new

        def whole(p, carry):
            keep(p, scores(p))
            return carry

        if far:
            lax.fori_loop(0, 2, whole, 0)
        else:
            lax.fori_loop(2 * h, quads, whole, 0)
            row = lax.broadcasted_iota(jnp.int32, (TILE, QUAD * RC), 0) % (TILE // 2) + (b * TOK + i * (TILE // 2))
            col = lax.broadcasted_iota(jnp.int32, (TILE, QUAD * RC), 1)
            col = col % RC + (col // RC) * TOK + (quads * QUAD * TOK + r * RC)
            keep(quads, jnp.where(col <= row, scores(quads), NEG))

    def unit_if_any(i, r, far):
        if far:
            pl.when(h == 1)(lambda: unit(i, r, far))
        else:
            unit(i, r, far)

    def values(i):
        final = top[i]

        def body(p, out):
            for r in range(R):
                e, f = sbuf[i, r, p], jnp.exp2(mbuf[i, r, p] - final)
                e = jnp.concatenate([e[:, j * RC : (j + 1) * RC] * f for j in range(QUAD)], axis=1)
                out = out + jnp.dot(
                    e.astype(jnp.bfloat16), quad_of(p, r, 1), preferred_element_type=jnp.float32
                )
            return out

        out = lax.fori_loop(0, quads + 1, body, jnp.zeros((TILE, HD), jnp.float32))
        out = (out / jnp.sum(lbuf[i], axis=1, keepdims=True)).astype(jnp.bfloat16)
        at = pl.ds(i * (TILE // 2), TILE // 2)
        abuf[at, 0:HD] = out[: TILE // 2]
        abuf[at, HD:] = out[TILE // 2 :]
        pltpu.make_async_copy(abuf.at[at], att_ref.at[at], a_sem.at[0]).start()

    own_hid.wait()
    for step in steps():
        what, number = step[0], step[1:]
        if what == "s":
            if XSEQ[int(number)][1] == 0:
                z_step(int(number))
            a_send(int(number))
        elif what == "z":
            if XSEQ[int(number)][1] > 0:
                z_step(int(number))
        elif what == "f":
            a_forward(int(number))
        elif what == "w":
            w_start("abc".index(number)) if number in "abc" else w_step(int(number))
        elif what == "q":
            for k in range(2):
                a_finish_last(k)
            project_last(0)
        elif what == "p" and int(number) == R - 1:
            for k in range(2, 4):
                a_finish_last(k)
            project_last(1)
            b_step(R - 1, "0", 0)
            b_step(R - 1, "0", 1)
            project_last(2)
        elif what == "p":
            if number == "0":
                load_wq.wait()
            a_finish(int(number))
            project(int(number))
            b_step(int(number), "0")
        elif what == "b":
            b_step(int(number[0]), number[2], "kv".index(number[3]) if number[3:] else 2)
        else:
            unit_if_any(int(number[2]), int(number[1]), "nf".index(number[0]))

    count = jnp.int32(0)
    index = [jnp.int32(0)] * CAP
    for bb in range(NB):
        hit = hosts_ref[routing_ref[bb]] == b
        for s in range(CAP):
            index[s] = jnp.where(hit & (count == s), bb, index[s])
        count = count + hit.astype(jnp.int32)
    for s in range(CAP):
        mine = kv[t % 2, index[s] // 8, (index[s] // 2) % 4, index[s] % 2]
        cbuf[s] = jnp.where(s < count, mine, jnp.zeros((TOK, HD), jnp.bfloat16))
    store_cache = pltpu.make_async_copy(cbuf, cache_ref, loc_sem.at[2])
    store_cache.start()

    for i in range(2):
        values(i)

    a_drain()
    w_drain()
    b_drain()
    store_cache.wait()
    pltpu.make_async_copy(abuf, att_ref, a_sem.at[0]).wait()


def hand_on(att_in, cache_in, att_out, cache_out, att, cache, sem_in, sem_out):
    parts = [(att_in, att, att_out, pl.ds(0, TOK))]
    parts += [(cache_in, cache, cache_out, pl.ds(2 * i, 2)) for i in range(CAP // 2)]
    loads = [pltpu.make_async_copy(a.at[at], v.at[at], sem_in.at[i]) for i, (a, v, _, at) in enumerate(parts)]
    stores = [pltpu.make_async_copy(v.at[at], o.at[at], sem_out.at[i]) for i, (_, v, o, at) in enumerate(parts)]
    for load in loads:
        load.start()
    for load, store in zip(loads, stores):
        load.wait()
        store.start()
    for store in stores:
        store.wait()


def local(hidden_in, w_query, w_keyval, routing, hosts):
    any_spec = pl.BlockSpec(memory_space=pl.ANY)
    smem = pl.BlockSpec(memory_space=pltpu.SMEM)
    dma = pltpu.SemaphoreType.DMA
    bf16, f32 = jnp.bfloat16, jnp.float32
    attended, cache = pl.pallas_call(
        kernel,
        out_shape=(
            jax.ShapeDtypeStruct((TOK, 2 * HD), bf16),
            jax.ShapeDtypeStruct((CAP, TOK, HD), bf16),
        ),
        in_specs=[any_spec, any_spec, any_spec, smem, smem],
        out_specs=(any_spec, any_spec),
        scratch_shapes=[
            pltpu.VMEM((4, 4, TOK, FD), bf16),
            pltpu.VMEM((NT, FD, 2 * HD), bf16),
            pltpu.VMEM((NT, 4, 2, PART, 2 * HD), bf16),
            pltpu.VMEM((2, 2, 4, 2, TOK, HD), bf16),
            pltpu.VMEM((2, RC, 2 * HD), f32),
            pltpu.VMEM((2 * TILE, HD), bf16),
            pltpu.VMEM((2, R, NB // QUAD, TILE, QUAD * RC), f32),
            pltpu.VMEM((2, R, NB // QUAD, TILE, HD), f32),
            pltpu.VMEM((2, TILE, HD), f32),
            pltpu.VMEM((2, TILE, HD), f32),
            pltpu.VMEM((TOK, 2 * HD), bf16),
            pltpu.VMEM((CAP, TOK, HD), bf16),
            dma((3,)),
            dma((4 * R,)), dma((2, 4)),
            dma((2, 4 * R)), dma((R + 3,)), dma((4,)),
            dma((1,)), dma((1,)),
            dma((1,)), dma((1,)),
            dma((1,)), dma((1,)),
            dma((R + 1, 2)), dma((1,)),
            dma((R + 1, 2)), dma((1,)),
            dma((R + 1,)), dma((1,)),
            dma((1,)),
        ],
        compiler_params=pltpu.CompilerParams(
            collective_id=0, has_side_effects=True, vmem_limit_bytes=60 * 1024 * 1024
        ),
        cost_estimate=pl.CostEstimate(flops=8 * 10**9, bytes_accessed=8 * 2**20, transcendentals=8 * 2**20),
    )(hidden_in, w_query.reshape(NT, FD, 2 * HD), w_keyval, routing.reshape(NB), hosts)
    attended, cache = pl.pallas_call(
        hand_on,
        out_shape=(
            jax.ShapeDtypeStruct((TOK, 2 * HD), bf16),
            jax.ShapeDtypeStruct((CAP, TOK, HD), bf16),
        ),
        in_specs=[any_spec, any_spec],
        out_specs=(any_spec, any_spec),
        scratch_shapes=[
            pltpu.VMEM((TOK, 2 * HD), bf16), pltpu.VMEM((CAP, TOK, HD), bf16),
            dma((1 + CAP // 2,)), dma((1 + CAP // 2,)),
        ],
    )(attended, cache)
    return attended, cache[None]


def solution(mesh):
    in_specs = (P("blk", "tp"), P(None, "tp"), P("tp", None), P(), P())
    out_specs = (P("blk", "tp"), P("blk", None, None, "tp"))
    return jax.shard_map(local, mesh=mesh, in_specs=in_specs, out_specs=out_specs, check_vma=False)
```

```python
import functools

import jax
import jax.numpy as jnp
from jax import lax
from jax.experimental import pallas as pl
from jax.experimental.pallas import tpu as pltpu
from jax.sharding import PartitionSpec as P

HEADS = 32
KVH = 8
HD = 128
TOK = 512
CAP = 8
NB = 16
NT = 16
FD = 256
PART = 32
R = 4
RC = TOK // R
HC = RC // 2
TILE = 2 * TOK // 2
QUAD = 4
MESH = pl.DeviceIdType.MESH
LOG2E = 1.4426950408889634
SCALE2 = HD**-0.5 * LOG2E
NEG = -1e30

XSEQ = [
    (0, 0), (1, 0), (0, 1), (1, 1), (0, 2), (2, 0), (0, 3), (1, 2),
    (1, 3), (3, 0), (2, 1), (2, 2), (2, 3), (3, 1), (3, 2), (3, 3),
]
LAG = 2


def steps():
    at = {
        0: ["wa", "wb", "wc"], 3: ["w0"], 9: ["w1"], 11: ["w2", "p0"], 13: ["p1"], 15: ["b0.1", "b0.n"],
    }
    order = ["s0"]
    for s in range(len(XSEQ)):
        if s > 0:
            order.append(f"s{s}")
        if s + 1 < len(XSEQ):
            order.append(f"z{s + 1}")
        if s >= LAG:
            order.append(f"f{s - LAG}")
        order += at.get(s, [])
    order += [f"f{s}" for s in range(len(XSEQ) - LAG, len(XSEQ) - 1)]
    order += ["b1.n", "b0.N", "un00", "p2", "b1.1", "b0.f", "b1.N", "un10", "b0.F", "uf00", "q3", "p3"]
    order += ["b2.n", "b2.1", "un01", "uf01", "b1.f", "b3.nk", "b3.nv", "un11", "b3.1k", "b3.1v", "b1.F", "uf10"]
    order += ["uf11", "b2.f", "b2.N", "b2.F", "un20", "un21", "b3.fk", "b3.fv", "b3.Nk", "un30", "un31", "b3.Nv"]
    order += ["b3.Fk", "uf20", "uf21", "uf30", "uf31", "b3.Fv"]
    return order


def kernel(
    hidden_ref, wq_ref, wkv_ref, routing_ref, hosts_ref,
    att_ref, cache_ref,
    hid, wq, wkv, kv, acc, qbuf, sbuf, mbuf, top, lbuf, abuf, cbuf,
    loc_sem, z_recv, z_send, x_recv, xh_recv, x_send,
    w_recv, w_send, wy_recv, wy_send, ws_recv, ws_send,
    y_recv, y_send, s_recv, s_send, c_recv, c_send, a_sem,
):
    b = lax.axis_index("blk")
    t = lax.axis_index("tp")
    c, y, h = b % 2, (b // 2) % 4, b // 8
    x, z = t % 4, t // 4
    part = b % 8
    xr, xl, xo = (x + 1) % 4, (x + 3) % 4, (x + 2) % 4
    yr, yl, yo = (y + 1) % 4, (y + 3) % 4, (y + 2) % 4
    dev_xr, dev_xl = (b, z * 4 + xr), (b, z * 4 + xl)
    dev_y = [(h * 8 + yy * 2 + c, t) for yy in (yr, yl, yo)]
    dev_xo = (b, z * 4 + xo)
    dev_sib = (b + 1 - 2 * c, t)
    dev_far = ((1 - h) * 8 + y * 2 + c, t)

    def rcopy(src, dst, ssem, rsem, dev):
        return pltpu.make_async_remote_copy(
            src_ref=src, dst_ref=dst, send_sem=ssem, recv_sem=rsem, device_id=dev, device_id_type=MESH
        )

    def recv(ref, rsem):
        rcopy(ref, ref, x_send.at[0], rsem, dev_xr).wait_recv()

    def sent(ref, ssem):
        rcopy(ref, ref, ssem, w_recv.at[0], dev_xr).wait_send()

    own_hid = pltpu.make_async_copy(hidden_ref, hid.at[z, x], loc_sem.at[0])
    own_hid.start()
    load_wq = pltpu.make_async_copy(wq_ref, wq, loc_sem.at[1])
    load_wq.start()

    top[...] = jnp.full(top.shape, NEG, jnp.float32)
    lbuf[...] = jnp.zeros_like(lbuf)

    barrier = pltpu.get_barrier_semaphore()

    def greet(dev):
        pl.semaphore_signal(barrier, inc=1, device_id=dev, device_id_type=MESH)

    def greet_tp(i, carry):
        greet((b, (t + i) % NT))
        return carry

    lax.fori_loop(1, NT, greet_tp, 0)
    for dev in (*dev_y, dev_sib, dev_far):
        greet(dev)
    pl.semaphore_wait(barrier, NT - 1 + 5)

    def rows(r):
        return pl.ds(r * RC, RC)

    def half(r, i):
        return pl.ds(r * RC + i * HC, HC)

    def zk(k):
        return (z, z + 1 - 2 * (z % 2), 2 - z // 2, 3 - 3 * (z // 2))[k]

    def piece_of(s):
        r, k = XSEQ[s]
        zp = zk(k)
        return r, zp, r * 4 + zp

    def z_step(s):
        r, zp, g = piece_of(s)
        ref = hid.at[zp, x, rows(r)]
        if XSEQ[s][1] > 0:
            recv(ref, z_recv.at[g])

        @pl.when((z < 3) & (zp <= z))
        def _():
            rcopy(ref, ref, z_send.at[0, zp], z_recv.at[g], (b, t + 4)).start()

        @pl.when((z > 0) & (zp >= z))
        def _():
            rcopy(ref, ref, z_send.at[1, zp], z_recv.at[g], (b, t - 4)).start()

    def a_send(s):
        r, zp, g = piece_of(s)
        ref = hid.at[zp, x, rows(r)]
        rcopy(ref, ref, x_send.at[0], x_recv.at[0, g], dev_xr).start()
        rcopy(ref, ref, x_send.at[1], x_recv.at[1, g], dev_xl).start()
        if s == len(XSEQ) - 1:
            rcopy(ref, ref, x_send.at[2], xh_recv.at[xh_of(s)], dev_xo).start()

    def xh_of(s):
        r, k = XSEQ[s]
        return r + k if r == R - 1 else r

    def a_forward(s):
        r, zp, g = piece_of(s)
        recv(hid.at[zp, xl, rows(r)], x_recv.at[0, g])
        ref = hid.at[zp, xl, half(r, 0)]
        rcopy(ref, ref, x_send.at[2], xh_recv.at[xh_of(s)], dev_xr).start()
        recv(hid.at[zp, xr, rows(r)], x_recv.at[1, g])
        ref = hid.at[zp, xr, half(r, 1)]
        rcopy(ref, ref, x_send.at[3], xh_recv.at[xh_of(s)], dev_xl).start()

    def a_finish(r):
        recv(hid.at[:, xo, rows(r)], xh_recv.at[r])

    def a_finish_last(k):
        recv(hid.at[zk(k), xo, rows(R - 1)], xh_recv.at[R - 1 + k])
        if k == 3:
            _, zp, g = piece_of(len(XSEQ) - 1)
            recv(hid.at[zp, xl, rows(R - 1)], x_recv.at[0, g])
            recv(hid.at[zp, xr, rows(R - 1)], x_recv.at[1, g])

    def a_drain():
        for kind in range(2):
            sent(hid.at[:, x], x_send.at[kind])
        sent(hid.at[pl.ds(0, 2), x], x_send.at[2])
        sent(hid.at[0, x, pl.ds(0, HC)], x_send.at[2])
        sent(hid.at[0, x], x_send.at[3])
        sent(hid.at[0, x, pl.ds(0, 3 * RC + HC)], x_send.at[3])
        for zp in range(4):
            @pl.when((z < 3) & (zp <= z))
            def _():
                sent(hid.at[zp, x], z_send.at[0, zp])

            @pl.when((z > 0) & (zp >= z))
            def _():
                sent(hid.at[zp, x], z_send.at[1, zp])

    def w_start(part_of):
        src_rows = pl.ds(part * PART, PART)

        def piece(to):
            return wkv_ref.at[src_rows, pl.ds(pl.multiple_of((to // 2) * 2 * HD, 2 * HD), 2 * HD)]

        def one(i, carry):
            to = (t + i) % NT
            rcopy(piece(to), wkv.at[t, y, c], w_send.at[0], w_recv.at[0], (b, to)).start()
            return carry

        if part_of == 0:
            pltpu.make_async_copy(piece(t), wkv.at[t, y, c], w_recv.at[0]).start()
        lax.fori_loop(1 + 5 * part_of, 6 + 5 * part_of, one, 0)

    def w_step(i):
        if i == 0:
            ref = wkv.at[:, y, c]
            recv(ref, w_recv.at[0])
            for j in range(3):
                rcopy(ref, ref, wy_send.at[0], wy_recv.at[0], dev_y[j]).start()
        elif i == 1:
            recv(wkv.at[:, pl.ds(0, 3), c], wy_recv.at[0])
            ref = wkv.at[:, :, c]
            rcopy(ref, ref, ws_send.at[0], ws_recv.at[0], dev_sib).start()
        else:
            recv(wkv.at[:, :, 1 - c], ws_recv.at[0])

    def w_drain():
        sent(wkv.at[pl.ds(0, NT - 1), y, c], w_send.at[0])
        sent(wkv.at[:, pl.ds(0, 3), c], wy_send.at[0])
        sent(wkv.at[:, :, c], ws_send.at[0])

    def product(r, zp, side):
        total = None
        for xp in range(4):
            rhs = wq[zp * 4 + xp] if side == 0 else wkv[zp * 4 + xp].reshape(FD, 2 * HD)
            one = jnp.dot(hid[zp, xp, rows(r)], rhs, preferred_element_type=jnp.float32)
            total = one if total is None else total + one
        return total

    def keep_keyval(r, total):
        for j in range(2):
            kv[j, h, y, c, rows(r)] = total[:, j * HD : (j + 1) * HD].astype(jnp.bfloat16)

    def keep_query(r, total):
        for head in range(2):
            at = (r // 2) * TILE + head * (TILE // 2) + (r % 2) * RC
            qbuf[pl.ds(at, RC)] = total[:, head * HD : (head + 1) * HD].astype(jnp.bfloat16)

    def project(r):
        acc[...] = jnp.zeros_like(acc)

        def body(zp, carry):
            for side in range(2):
                acc[side] += product(r, zp, side)
            return carry

        lax.fori_loop(0, 4, body, 0)
        keep_keyval(r, acc[1])
        keep_query(r, acc[0])

    def project_last(part):
        r = R - 1
        if part == 0:
            for side in range(2):
                acc[side] = product(r, zk(0), side) + product(r, zk(1), side)
        elif part == 1:
            keep_keyval(r, acc[1] + product(r, zk(2), 1) + product(r, zk(3), 1))
        else:
            keep_query(r, acc[0] + product(r, zk(2), 0) + product(r, zk(3), 0))

    def sides(part):
        return pl.ds(0, 2) if part == 2 else pl.ds(part, 1)

    def slot(r, part):
        return R if part == 1 else r

    def b_send(r, part, far):
        ref = kv.at[sides(part), (h + far) % 2, y, c, rows(r)]
        for j in range(3):
            rcopy(ref, ref, y_send.at[0], y_recv.at[slot(r, part), far], dev_y[j]).start()

    def b_share(r, part, far):
        hh = (h + far) % 2
        recv(kv.at[sides(part), hh, pl.ds(0, 3), c, rows(r)], y_recv.at[slot(r, part), far])
        ref = kv.at[sides(part), hh, :, c, rows(r)]
        rcopy(ref, ref, s_send.at[0], s_recv.at[slot(r, part), far], dev_sib).start()

    def b_step(r, what, part=2):
        at = slot(r, part)
        if what == "0":
            ref = kv.at[sides(part), h, y, c, rows(r)]
            rcopy(ref, ref, c_send.at[0], c_recv.at[at], dev_far).start()
            b_send(r, part, 0)
        elif what == "1":
            recv(kv.at[sides(part), 1 - h, y, c, rows(r)], c_recv.at[at])
            b_send(r, part, 1)
        elif what in "nf":
            b_share(r, part, "nf".index(what))
        else:
            far = "NF".index(what)
            recv(kv.at[sides(part), (h + far) % 2, :, 1 - c, rows(r)], s_recv.at[at, far])

    def b_drain():
        sent(kv.at[:, 0, pl.ds(0, 3)], y_send.at[0])
        sent(kv.at[:, :, :, 0], s_send.at[0])
        sent(kv.at[:, 0, 0, 0], c_send.at[0])

    quads = b // QUAD

    def quad_of(p, r, first):
        return kv[first, p // 2, pl.ds((p % 2) * 2, 2), :, rows(r)].reshape(QUAD * RC, HD)

    def unit(i, r, far):
        q = qbuf[pl.ds(i * TILE, TILE)]

        def scores(p):
            return SCALE2 * lax.dot_general(
                q, quad_of(p, r, 0), (((1,), (1,)), ((), ())), preferred_element_type=jnp.float32
            )

        def keep(p, s):
            s = [s[:, j * RC : (j + 1) * RC] for j in range(QUAD)]
            m = jnp.maximum(jnp.maximum(s[0], s[1]), jnp.maximum(s[2], s[3]))
            m = jnp.broadcast_to(jnp.max(m, axis=1, keepdims=True), (TILE, HD))
            mbuf[i, r, p] = m
            e = [jnp.exp2(one - m) for one in s]
            sbuf[i, r, p] = jnp.concatenate(e, axis=1)
            old = top[i]
            new = jnp.maximum(old, m)
            lbuf[i] = lbuf[i] * jnp.exp2(old - new) + ((e[0] + e[1]) + (e[2] + e[3])) * jnp.exp2(m - new)
            top[i] = new

        def whole(p, carry):
            keep(p, scores(p))
            return carry

        if far:
            lax.fori_loop(0, 2, whole, 0)
        else:
            lax.fori_loop(2 * h, quads, whole, 0)
            row = lax.broadcasted_iota(jnp.int32, (TILE, QUAD * RC), 0) % (TILE // 2) + (b * TOK + i * (TILE // 2))
            col = lax.broadcasted_iota(jnp.int32, (TILE, QUAD * RC), 1)
            col = col % RC + (col // RC) * TOK + (quads * QUAD * TOK + r * RC)
            keep(quads, jnp.where(col <= row, scores(quads), NEG))

    def unit_if_any(i, r, far):
        if far:
            pl.when(h == 1)(lambda: unit(i, r, far))
        else:
            unit(i, r, far)

    def values(i):
        final = top[i]

        def body(p, out):
            for r in range(R):
                e, f = sbuf[i, r, p], jnp.exp2(mbuf[i, r, p] - final)
                e = jnp.concatenate([e[:, j * RC : (j + 1) * RC] * f for j in range(QUAD)], axis=1)
                out = out + jnp.dot(
                    e.astype(jnp.bfloat16), quad_of(p, r, 1), preferred_element_type=jnp.float32
                )
            return out

        out = lax.fori_loop(0, quads + 1, body, jnp.zeros((TILE, HD), jnp.float32))
        out = (out / jnp.sum(lbuf[i], axis=1, keepdims=True)).astype(jnp.bfloat16)
        at = pl.ds(i * (TILE // 2), TILE // 2)
        abuf[at, 0:HD] = out[: TILE // 2]
        abuf[at, HD:] = out[TILE // 2 :]
        pltpu.make_async_copy(abuf.at[at], att_ref.at[at], a_sem.at[0]).start()

    own_hid.wait()
    for step in steps():
        what, number = step[0], step[1:]
        if what == "s":
            if XSEQ[int(number)][1] == 0:
                z_step(int(number))
            a_send(int(number))
        elif what == "z":
            if XSEQ[int(number)][1] > 0:
                z_step(int(number))
        elif what == "f":
            a_forward(int(number))
        elif what == "w":
            w_start("abc".index(number)) if number in "abc" else w_step(int(number))
        elif what == "q":
            for k in range(2):
                a_finish_last(k)
            project_last(0)
        elif what == "p" and int(number) == R - 1:
            for k in range(2, 4):
                a_finish_last(k)
            project_last(1)
            b_step(R - 1, "0", 0)
            b_step(R - 1, "0", 1)
            project_last(2)
        elif what == "p":
            if number == "0":
                load_wq.wait()
            a_finish(int(number))
            project(int(number))
            b_step(int(number), "0")
        elif what == "b":
            b_step(int(number[0]), number[2], "kv".index(number[3]) if number[3:] else 2)
        else:
            unit_if_any(int(number[2]), int(number[1]), "nf".index(number[0]))

    count = jnp.int32(0)
    index = [jnp.int32(0)] * CAP
    for bb in range(NB):
        hit = hosts_ref[routing_ref[bb]] == b
        for s in range(CAP):
            index[s] = jnp.where(hit & (count == s), bb, index[s])
        count = count + hit.astype(jnp.int32)
    for s in range(CAP):
        mine = kv[t % 2, index[s] // 8, (index[s] // 2) % 4, index[s] % 2]
        cbuf[s] = jnp.where(s < count, mine, jnp.zeros((TOK, HD), jnp.bfloat16))
    store_cache = pltpu.make_async_copy(cbuf, cache_ref, loc_sem.at[2])
    store_cache.start()

    for i in range(2):
        values(i)

    a_drain()
    w_drain()
    b_drain()
    store_cache.wait()
    pltpu.make_async_copy(abuf, att_ref, a_sem.at[0]).wait()


def hand_on(att_in, cache_in, att_out, cache_out, att, cache, sem_in, sem_out):
    parts = [(att_in, att, att_out, pl.ds(0, TOK))]
    parts += [(cache_in, cache, cache_out, pl.ds(2 * i, 2)) for i in range(CAP // 2)]
    loads = [pltpu.make_async_copy(a.at[at], v.at[at], sem_in.at[i]) for i, (a, v, _, at) in enumerate(parts)]
    stores = [pltpu.make_async_copy(v.at[at], o.at[at], sem_out.at[i]) for i, (_, v, o, at) in enumerate(parts)]
    for load in loads:
        load.start()
    for load, store in zip(loads, stores):
        load.wait()
        store.start()
    for store in stores:
        store.wait()


def local(hidden_in, w_query, w_keyval, routing, hosts):
    any_spec = pl.BlockSpec(memory_space=pl.ANY)
    smem = pl.BlockSpec(memory_space=pltpu.SMEM)
    dma = pltpu.SemaphoreType.DMA
    bf16, f32 = jnp.bfloat16, jnp.float32
    attended, cache = pl.pallas_call(
        kernel,
        out_shape=(
            jax.ShapeDtypeStruct((TOK, 2 * HD), bf16),
            jax.ShapeDtypeStruct((CAP, TOK, HD), bf16),
        ),
        in_specs=[any_spec, any_spec, any_spec, smem, smem],
        out_specs=(any_spec, any_spec),
        scratch_shapes=[
            pltpu.VMEM((4, 4, TOK, FD), bf16),
            pltpu.VMEM((NT, FD, 2 * HD), bf16),
            pltpu.VMEM((NT, 4, 2, PART, 2 * HD), bf16),
            pltpu.VMEM((2, 2, 4, 2, TOK, HD), bf16),
            pltpu.VMEM((2, RC, 2 * HD), f32),
            pltpu.VMEM((2 * TILE, HD), bf16),
            pltpu.VMEM((2, R, NB // QUAD, TILE, QUAD * RC), f32),
            pltpu.VMEM((2, R, NB // QUAD, TILE, HD), f32),
            pltpu.VMEM((2, TILE, HD), f32),
            pltpu.VMEM((2, TILE, HD), f32),
            pltpu.VMEM((TOK, 2 * HD), bf16),
            pltpu.VMEM((CAP, TOK, HD), bf16),
            dma((3,)),
            dma((4 * R,)), dma((2, 4)),
            dma((2, 4 * R)), dma((R + 3,)), dma((4,)),
            dma((1,)), dma((1,)),
            dma((1,)), dma((1,)),
            dma((1,)), dma((1,)),
            dma((R + 1, 2)), dma((1,)),
            dma((R + 1, 2)), dma((1,)),
            dma((R + 1,)), dma((1,)),
            dma((1,)),
        ],
        compiler_params=pltpu.CompilerParams(
            collective_id=0, has_side_effects=True, vmem_limit_bytes=60 * 1024 * 1024
        ),
        cost_estimate=pl.CostEstimate(flops=8 * 10**9, bytes_accessed=8 * 2**20, transcendentals=8 * 2**20),
    )(hidden_in, w_query.reshape(NT, FD, 2 * HD), w_keyval, routing.reshape(NB), hosts)
    attended, cache = pl.pallas_call(
        hand_on,
        out_shape=(
            jax.ShapeDtypeStruct((TOK, 2 * HD), bf16),
            jax.ShapeDtypeStruct((CAP, TOK, HD), bf16),
        ),
        in_specs=[any_spec, any_spec],
        out_specs=(any_spec, any_spec),
        scratch_shapes=[
            pltpu.VMEM((TOK, 2 * HD), bf16), pltpu.VMEM((CAP, TOK, HD), bf16),
            dma((1 + CAP // 2,)), dma((1 + CAP // 2,)),
        ],
    )(attended, cache)
    return attended, cache[None]


def solution(mesh):
    in_specs = (P("blk", "tp"), P(None, "tp"), P("tp", None), P(), P())
    out_specs = (P("blk", "tp"), P("blk", None, None, "tp"))
    return jax.shard_map(local, mesh=mesh, in_specs=in_specs, out_specs=out_specs, check_vma=False)
```
